128 devices in a mesh: exc: 4 (over y_lo, core), space: 32 (over x, y_hi, z).
Axes of the slice: x: 4, y: 4 (y_hi: 2, y_lo: 2; y = y_hi * 2 + y_lo), z: 4, core: 2. Of those that a mesh axis runs over, the one named last changes fastest.
Arguments:
- forward_fields: float32 [4, 6, 32, 256, 1024], P('exc', None, None, 'space'), may hold values from -6 to 6
- forward_sums: float32 [4, 6, 8, 256, 1024], P('exc', None, None, 'space'), may hold values from -6 to 6
- adjoint_fields: float32 [4, 6, 32, 256, 1024], P('exc', None, None, 'space'), may hold values from -6 to 6
- adjoint_sums: float32 [4, 6, 8, 256, 1024], P('exc', None, None, 'space'), may hold values from -6 to 6
- monitor_sums: float32 [4, 2, 32, 256], P('exc', None, None, 'space'), may hold values from -6 to 6
- density: float32 [1024, 256], P('exc', 'space'), may hold values from 0 to 1
- labels: int32 [256, 1024], P('space'), may hold values from 0 to 2
- source_plane: int32 [4], P('exc'), may hold values from 0 to 1023
- monitor_plane: int32 [4], P('exc'), may hold values from 0 to 1023
- mode_numbers: int32 [4], P('exc'), may hold values from 0 to 3
- frequency: float32 [4], P('exc'), may hold values from 0.3 to 1.2
- start_phase: float32 [4], P('exc'), may hold values from -3.140625 to 3.140625
Outputs:
- design_gradient: float32 [1024, 256], P('exc', 'space')
- figure_of_merit: float32 [4], P('exc')
The draws below stay inside these ranges and needn't reach their ends.
All inputs are finite; a program needn't handle non-finite values.
Results may differ from the reference program's by a relative error of at most 0.0003.
Values sent between devices are 32-bit elements; how exact they have to be, the bound alone decides.
No kernel may reach another device: no remote copies, remote signals or barrier semaphores. Data moves between devices by JAX's collectives and lax.ppermute only.
A program may use at most 128 MiB of HBM per device.

```python
import math
import jax
import jax.numpy as jnp
from jax import lax

NX = 1024
NZ = 32
DZ = 8
STEPS = 2
R = 4
NY = 256
EXC = 4


def plant(values, rng, smallest, high):
    dims = values.shape
    spot = [jax.random.randint(jax.random.fold_in(rng, axis), (), 0, dims[axis]) for axis in range(len(dims))]
    values = values.at[tuple(spot)].set(smallest)
    longest = dims.index(max(dims))
    spot[longest] = (spot[longest] + 1) % dims[longest]
    return values.at[tuple(spot)].set(high)


def block_scale(key, extent, shards, low, largest):
    factor_of = 1.0
    for dim, shards_of in shards:
        steps = jax.random.uniform(jax.random.fold_in(jax.random.fold_in(key, 6), dim), (shards_of,), jnp.float32, low / len(shards), largest / len(shards))
        factor_of = factor_of * jnp.repeat(jnp.exp(steps), extent[dim] // shards_of).reshape((-1,) + (1,) * (len(extent) - 1 - dim))
    return factor_of


def centred(own_key, shape, deviation, reach, cuts=(), kind=jnp.bfloat16):
    array = deviation * jax.random.normal(own_key, shape, jnp.float32)
    if cuts:
        array = array * block_scale(own_key, shape, cuts, -0.22, 0.18)
    return jnp.clip(array, -reach, reach).astype(kind)


def setup_inputs(seed: int = 0) -> dict:
    streams_of = jax.random.split(jax.random.key(seed), 13)
    return {
        "forward_fields": centred(streams_of[0], (EXC, 6, NZ, NY, NX), 1.0, 6.0, ((0, 4), (3, 32)), jnp.float32),
        "forward_sums": centred(streams_of[1], (EXC, 6, DZ, NY, NX), 1.0, 6.0, ((0, 4), (3, 32)), jnp.float32),
        "adjoint_fields": centred(streams_of[2], (EXC, 6, NZ, NY, NX), 1.0, 6.0, ((0, 4), (3, 32)), jnp.float32),
        "adjoint_sums": centred(streams_of[3], (EXC, 6, DZ, NY, NX), 1.0, 6.0, ((0, 4), (3, 32)), jnp.float32),
        "monitor_sums": centred(streams_of[4], (EXC, 2, NZ, NY), 1.0, 6.0, ((0, 4), (3, 32)), jnp.float32),
        "density": jnp.clip(1.0 * jax.random.uniform(streams_of[5], (NX, NY), jnp.float32) ** block_scale(streams_of[5], (NX, NY), ((0, 4), (1, 32)), -0.2, 0.2), 0.0, 1.0),
        "labels": plant(jax.random.randint(streams_of[6], (NY, NX), 0, 3), jax.random.fold_in(streams_of[6], 1), 0, 2).astype(jnp.int32),
        "source_plane": plant(jax.random.randint(streams_of[7], (EXC,), 0, NX), jax.random.fold_in(streams_of[7], 1), 0, NX - 1).astype(jnp.int32),
        "monitor_plane": plant(jax.random.randint(streams_of[8], (EXC,), 0, NX), jax.random.fold_in(streams_of[8], 1), 0, NX - 1).astype(jnp.int32),
        "mode_numbers": plant(jax.random.randint(streams_of[9], (EXC,), 0, 4), jax.random.fold_in(streams_of[9], 1), 0, 3).astype(jnp.int32),
        "frequency": jnp.clip(jnp.exp(math.log(1.2) - 1.3862944 * jax.random.uniform(streams_of[10], (EXC,), jnp.float32) ** block_scale(streams_of[10], (EXC,), ((0, 4),), -0.2, 0.2)), 0.3, 1.2),
        "start_phase": jnp.clip(jax.random.uniform(streams_of[11], (EXC,), jnp.float32, -3.140625, 3.140625), -3.140625, 3.140625),
    }


COURANT = 0.5
OXIDE_PERMITTIVITY = 2.1
SILICON_PERMITTIVITY = 12.1
AIR_PERMITTIVITY = 1.0
SHARPNESS = 4.0
MIDPOINT = 0.5

def smooth(padded, radius):
    row_total = padded.shape[0] - 2 * radius
    column_total = padded.shape[1] - 2 * radius
    across = None
    for offset in range(2 * radius + 1):
        weight = (radius + 1.0 - abs(offset - radius)) / ((radius + 1.0) * (radius + 1.0))
        addend = weight * padded[:, offset:offset + column_total]
        across = addend if across is None else across + addend
    result = None
    for offset in range(2 * radius + 1):
        weight = (radius + 1.0 - abs(offset - radius)) / ((radius + 1.0) * (radius + 1.0))
        addend = weight * across[offset:offset + row_total, :]
        result = addend if result is None else result + addend
    return result

def project(filtered):
    lower = math.tanh(SHARPNESS * MIDPOINT)
    spread = lower + math.tanh(SHARPNESS * (1.0 - MIDPOINT))
    bent = jnp.tanh(SHARPNESS * (filtered - MIDPOINT))
    return ((lower + bent) / spread, SHARPNESS * (1.0 - bent * bent) / spread)

def slab_inverse(labels, projected):
    material = jnp.where(labels == 1, SILICON_PERMITTIVITY, OXIDE_PERMITTIVITY)
    mixed = OXIDE_PERMITTIVITY + (SILICON_PERMITTIVITY - OXIDE_PERMITTIVITY) * projected
    return 1.0 / jnp.where(labels == 2, mixed, material)

def layered(inverse_rows, layer_count, slab_start, slab_layers):
    row_total, column_total = inverse_rows.shape
    beneath = jnp.full((slab_start, row_total, column_total), 1.0 / OXIDE_PERMITTIVITY, jnp.float32)
    middle = jnp.broadcast_to(inverse_rows[None], (slab_layers, row_total, column_total))
    overhead = jnp.full((layer_count - slab_start - slab_layers, row_total, column_total), 1.0 / AIR_PERMITTIVITY, jnp.float32)
    return jnp.concatenate((beneath, middle, overhead), 0)

def profile(modes, rows, layer_count, grid_rows):
    layers = jnp.arange(layer_count, dtype=jnp.float32) + 0.5
    order = (modes + 1).astype(jnp.float32)
    across_z = jnp.sin(math.pi * order[:, None] * layers[None, :] / layer_count)
    ramp = 1.0 + 2.0 * (rows + 0.5) / grid_rows
    return across_z[:, :, None] * ramp[None, None, :]

def upward(field, axis):
    size = field.shape[axis]
    later = jnp.concatenate((lax.slice_in_dim(field, 1, size, axis=axis), jnp.zeros_like(lax.slice_in_dim(field, 0, 1, axis=axis))), axis)
    return later - field

def downward(field, axis):
    size = field.shape[axis]
    earlier = jnp.concatenate((jnp.zeros_like(lax.slice_in_dim(field, 0, 1, axis=axis)), lax.slice_in_dim(field, 0, size - 1, axis=axis)), axis)
    return field - earlier

def advance(fields, sums, inverse, shape, plane, cosine_weight, sine_weight, phase_start, rate, watched, column_ids):
    slab_start = (NZ - DZ) // 2
    electric_x, electric_y, electric_z = (fields[0], fields[1], fields[2])
    magnetic_x, magnetic_y, magnetic_z = (fields[3], fields[4], fields[5])
    column_mask = (column_ids == plane).astype(jnp.float32)
    for step_index in range(STEPS):
        phase_now = phase_start + rate * step_index
        cosine = jnp.cos(phase_now)
        sine_part = jnp.sin(phase_now)
        strength = cosine_weight * cosine + sine_weight * sine_part
        magnetic_x = magnetic_x - COURANT * (upward(electric_z, 1) - upward(electric_y, 0))
        magnetic_y = magnetic_y - COURANT * (upward(electric_x, 0) - upward(electric_z, 2))
        magnetic_z = magnetic_z - COURANT * (upward(electric_y, 2) - upward(electric_x, 1))
        source = (shape * strength)[:, :, None] * column_mask[None, None, :]
        electric_x = electric_x + COURANT * inverse * (downward(magnetic_z, 1) - downward(magnetic_y, 0))
        electric_y = electric_y + COURANT * inverse * (downward(magnetic_x, 0) - downward(magnetic_z, 2))
        electric_z = electric_z + COURANT * inverse * (downward(magnetic_y, 2) - downward(magnetic_x, 1) - source)
        recorded = jnp.stack((electric_x, electric_y, electric_z), 0)[:, slab_start:slab_start + DZ]
        sums = jnp.concatenate((sums[:3] + recorded * cosine, sums[3:] - recorded * sine_part), 0)
        if watched is not None:
            column = lax.dynamic_index_in_dim(electric_z, plane, 2, keepdims=False)
            watched = jnp.stack((watched[0] + column * cosine, watched[1] - column * sine_part), 0)
    return (sums, watched)

def reference(forward_fields, forward_sums, adjoint_fields, adjoint_sums, monitor_sums, density, labels, source_plane, monitor_plane, mode_numbers, frequency, start_phase):
    filtered = smooth(jnp.pad(density, R), R).T
    projected, steepness = project(filtered)
    inverse = layered(slab_inverse(labels, projected), NZ, (NZ - DZ) // 2, DZ)
    shapes = profile(mode_numbers, jnp.arange(NY, dtype=jnp.float32), NZ, NY)
    column_ids = jnp.arange(NX, dtype=jnp.int32)
    norm_factor = math.sqrt(NZ * NY)

    def one_source(items):
        fields_ahead, sums_ahead, fields_back, sums_back, watched, plane_ahead, plane_back, shape, rate, phase_start = items
        sums_ahead, watched = advance(fields_ahead, sums_ahead, inverse, shape, plane_ahead, 1.0, 0.0, phase_start, rate, watched, column_ids)
        intersection_real = jnp.sum(watched[0] * shape) / norm_factor
        intersection_imaginary = jnp.sum(watched[1] * shape) / norm_factor
        sums_back, unused = advance(fields_back, sums_back, inverse, shape, plane_back, intersection_real, intersection_imaginary, phase_start, rate, None, column_ids)
        product = sums_ahead[:3] * sums_back[:3] - sums_ahead[3:] * sums_back[3:]
        merit = intersection_real * intersection_real + intersection_imaginary * intersection_imaginary
        return (merit, rate * rate * lax.optimization_barrier(jnp.sum(product, axis=(0, 1))))
    merits, gradients = lax.map(one_source, (forward_fields, forward_sums, adjoint_fields, adjoint_sums, monitor_sums, source_plane, monitor_plane, shapes, frequency, start_phase))
    design = (labels == 2).astype(jnp.float32)
    scale = 1.0 / math.sqrt(EXC * DZ)
    sensitivity = lax.optimization_barrier(jnp.sum(gradients, axis=0)) * (scale * (SILICON_PERMITTIVITY - OXIDE_PERMITTIVITY)) * design * steepness
    design_gradient = smooth(jnp.pad(sensitivity.T, R), R)
    return (design_gradient, merits)
```

```python
import math

import jax
import jax.numpy as jnp
from jax import lax
from jax.experimental import pallas as pl
from jax.experimental.pallas import tpu as pltpu
from jax.sharding import PartitionSpec as P

R = 4
COURANT = 0.5
OXIDE = 2.1
SILICON = 12.1
SHARPNESS = 4.0
MIDPOINT = 0.5

ROWS = 8
NX = 1024
NZ = 32
SLAB = 12
DZ = 8
UP_ROWS = 64
DOWN_ROWS = 40
PACK = 16 + 2 * UP_ROWS
WEIGHTS = [(R + 1.0 - abs(k - R)) / ((R + 1.0) * (R + 1.0)) for k in range(2 * R + 1)]
VMEM_LIMIT = 50 * 1024 * 1024

SMEM_SPEC = pl.BlockSpec(memory_space=pltpu.SMEM)
VMEM_SPEC = pl.BlockSpec(memory_space=pltpu.VMEM)
ANY_SPEC = pl.BlockSpec(memory_space=pl.ANY)


def slot(z):
    return (z - SLAB) % 16


def lanes(shape):
    return lax.broadcasted_iota(jnp.int32, shape, len(shape) - 1)


def sublanes(shape):
    return lax.broadcasted_iota(jnp.int32, shape, len(shape) - 2)


def x_up(f):
    n = f.shape[-1]
    return jnp.where(lanes(f.shape) == n - 1, 0.0, pltpu.roll(f, n - 1, len(f.shape) - 1))


def x_down(f):
    return jnp.where(lanes(f.shape) == 0, 0.0, pltpu.roll(f, 1, len(f.shape) - 1))


def roll_up(f):
    return pltpu.roll(f, f.shape[0] - 1, 0)


def roll_down(f):
    return pltpu.roll(f, 1, 0)


def y_smooth(f, count):
    total = None
    for k, w in enumerate(WEIGHTS):
        part = w * f[k : k + count]
        total = part if total is None else total + part
    return total


def x_smooth(f):
    n = f.shape[-1]
    ids = lanes(f.shape)
    total = WEIGHTS[R] * f
    for a in range(1, R + 1):
        ahead = jnp.where(ids < n - a, pltpu.roll(f, n - a, 1), 0.0)
        behind = jnp.where(ids >= a, pltpu.roll(f, a, 1), 0.0)
        total = total + WEIGHTS[R + a] * (ahead + behind)
    return total


def pack_kernel(ip, ff, af, dens, lab, ev, od, rows, up, down, sem, out_sem):
    copies = []
    for p, f in enumerate((ff, af)):
        for k, r in enumerate((0, 1, 6, 7)):
            copies.append(pltpu.make_async_copy(f.at[0, :, 8:24, r, :], rows.at[p, k], sem.at[p, k]))
    for c in copies:
        c.start()
    own = lab[...].astype(jnp.float32)
    up[0:8] = dens[...]
    up[8:16] = own
    down[0:8] = dens[...]
    down[8:16] = own
    tile = sublanes((8, NX))
    for p in range(2):
        for k in range(4):
            copies[4 * p + k].wait()

        def row(k, c, p=p):
            return pltpu.roll(rows[p, k, c], 12, 0)

        ex, ey, ez = row(0, 0), row(0, 1), row(0, 2)
        ex_n, ez_n = row(1, 0), row(1, 2)
        hx = row(0, 3) - COURANT * ((ez_n - ez) - (roll_up(ey) - ey))
        hy = row(0, 4) - COURANT * ((roll_up(ex) - ex) - (x_up(ez) - ez))
        hz = row(0, 5) - COURANT * ((x_up(ey) - ey) - (ex_n - ex))
        cx = hz - (hy - roll_down(hy))
        cz = (hy - x_down(hy)) - hx
        base = 16 + p * DOWN_ROWS
        down[base : base + 8] = ex[0:8]
        down[base + 8 : base + 16] = ez[0:8]
        down[base + 16 : base + 24] = cx[0:8]
        down[base + 24 : base + 32] = cz[0:8]
        extra = jnp.where((tile == 1) | (tile == 2), pltpu.roll(ex[8:16], 2, 0), ez[8:16])
        down[base + 32 : base + 40] = jnp.where(tile == 3, pltpu.roll(cz[8:16], 4, 0), extra)

        ex_l, ey_l, ez_l = row(2, 0), row(2, 1), row(2, 2)
        ex, ey, ez = row(3, 0), row(3, 1), row(3, 2)
        u1 = (x_up(ey) - ey) + ex
        u2 = ez + (roll_up(ey) - ey)
        hx = row(3, 3) + COURANT * u2
        hy = row(3, 4) - COURANT * ((roll_up(ex) - ex) - (x_up(ez) - ez))
        hz = row(3, 5) - COURANT * u1
        hx_l = row(2, 3) - COURANT * ((ez - ez_l) - (roll_up(ey_l) - ey_l))
        hz_l = row(2, 5) - COURANT * ((x_up(ey_l) - ey_l) - (ex - ex_l))
        cx = (hz - hz_l) - (hy - roll_down(hy))
        cy = (hx - roll_down(hx)) - (hz - x_down(hz))
        cz = (hy - x_down(hy)) - (hx - hx_l)
        base = 16 + p * UP_ROWS
        for k, v in enumerate((hx, hz, u1, u2, cx, cy, cz)):
            up[base + 8 * k : base + 8 * k + 8] = v[0:8]
        extra = jnp.where((tile == 1) | (tile == 2), pltpu.roll(hz[8:16], 2, 0), hx[8:16])
        up[base + 56 : base + 64] = jnp.where(tile == 3, pltpu.roll(cy[8:16], 3, 0), extra)

    even = ip[0] % 2 == 0

    def send(to_up, to_down):
        a = pltpu.make_async_copy(up, to_up, out_sem.at[0])
        b = pltpu.make_async_copy(down, to_down.at[0 : 16 + 2 * DOWN_ROWS], out_sem.at[1])
        a.start()
        b.start()
        a.wait()
        b.wait()

    @pl.when(even)
    def _():
        send(ev, od)

    @pl.when(jnp.logical_not(even))
    def _():
        send(od, ev)


def from_neighbours(ip, ev, od, below, above, below_rows, above_rows, sem):
    even = ip[0] % 2 == 0

    def get(from_below, from_above):
        a = pltpu.make_async_copy(from_below.at[below_rows], below, sem.at[0])
        b = pltpu.make_async_copy(from_above.at[above_rows], above, sem.at[1])
        a.start()
        b.start()
        a.wait()
        b.wait()

    @pl.when(even)
    def _():
        get(od, ev)

    @pl.when(jnp.logical_not(even))
    def _():
        get(ev, od)


def cyclic_rows(shape):
    i = sublanes(shape)
    return jnp.where(i < 12, i, i - 16)


def window_start(first):
    return pl.multiple_of(jnp.clip((first // 128) * 128, 0, NX - 256), 128)


def layer_inverse(z, middle):
    if z < SLAB:
        return 1.0 / OXIDE
    if z >= SLAB + DZ:
        return 1.0
    return middle


def material_kernel(
    grid_rows, ip, fp, ev, od, dens, lab, monitor, shape_zy, ff, inv_out, design_out, part_out,
    below, above, fw, sem, win_sem,
):
    strip, plane = ip[0], ip[1]
    w0 = window_start(plane - 2)
    window = pltpu.make_async_copy(ff.at[0, :, :, :, pl.ds(w0, 256)], fw, win_sem)
    window.start()
    from_neighbours(ip, ev, od, below, above, pl.ds(0, 16), pl.ds(0, 16), sem)
    own = lab[...].astype(jnp.float32)
    wide = jnp.concatenate([below[0:8], dens[...], above[0:8]], 0)
    kinds = jnp.concatenate([below[8:16], own, above[8:16]], 0)[4:20]
    filtered = x_smooth(y_smooth(wide, 16))
    lower = math.tanh(SHARPNESS * MIDPOINT)
    spread = lower + math.tanh(SHARPNESS * (1.0 - MIDPOINT))
    bent = jnp.tanh(SHARPNESS * (filtered - MIDPOINT))
    projected = (lower + bent) / spread
    steepness = SHARPNESS * (1.0 - bent * bent) / spread
    mixed = OXIDE + (SILICON - OXIDE) * projected
    material = jnp.where(kinds == 2.0, mixed, jnp.where(kinds == 1.0, SILICON, OXIDE))
    inv_out[...] = pltpu.roll(1.0 / material, 12, 0)
    design = jnp.where(kinds == 2.0, steepness * fp[36], 0.0)
    design_out[...] = pltpu.roll(design, 12, 0)[0:8]

    small = (16, 128)
    shift = (64 + w0 - plane + 256) % 256
    middle = pltpu.roll(inv_out[:, pl.ds(w0, 256)], shift, 1)[:, 0:128]
    rows_here = cyclic_rows(small) + ROWS * strip
    xs = lanes(small) + (plane - 64)
    inside = (rows_here >= 0) & (rows_here < grid_rows) & (xs >= 0) & (xs < NX)
    mask = jnp.where(inside, 1.0, 0.0)
    half = COURANT * mask
    ramp = 1.0 + 2.0 * (rows_here.astype(jnp.float32) + 0.5) / grid_rows
    seed_base = jnp.where(lanes(small) == 64, ramp * mask, 0.0)
    source_base = jnp.where(lanes(small) == 64, ramp, 0.0)[0:8]
    zero = jnp.zeros(small, jnp.float32)

    def at(values, z):
        return values[z] if 0 <= z < NZ else zero

    def xu(v):
        return pltpu.roll(v, 127, 1)

    def xd(v):
        return pltpu.roll(v, 1, 1)

    zs = range(NZ)
    inv = [layer_inverse(z, middle) for z in zs]
    seed = [seed_base * fp[z] for z in zs]
    w = [inv[z] * seed[z] for z in zs]
    hx = [half * (roll_up(w[z]) - w[z]) for z in zs]
    hy = [half * (w[z] - xu(w[z])) for z in zs]
    ex = [half * (hy[z] - at(hy, z - 1)) for z in zs]
    ey = [half * (at(hx, z - 1) - hx[z]) for z in zs]
    ez = [
        (seed[z] - COURANT * ((hy[z] - xd(hy[z])) - (hx[z] - roll_down(hx[z])))) * mask for z in zs
    ]
    wx = [inv[z] * ex[z] for z in zs]
    wy = [inv[z] * ey[z] for z in zs]
    wz = [inv[z] * ez[z] for z in zs]
    hx2 = [hx[z] + half * ((roll_up(wz[z]) - wz[z]) - (at(wy, z + 1) - wy[z])) for z in zs]
    hy2 = [hy[z] + half * ((at(wx, z + 1) - wx[z]) - (xu(wz[z]) - wz[z])) for z in zs]
    hz2 = [half * ((xu(wy[z]) - wy[z]) - (roll_up(wx[z]) - wx[z])) for z in zs]
    window.wait()
    one = jnp.zeros((8, 128), jnp.float32)
    two = jnp.zeros((8, 128), jnp.float32)
    c0, s0, c1, s1 = fp[32], fp[33], fp[34], fp[35]
    for z in zs:
        ex2 = ex[z] - half * (
            (hz2[z] - roll_down(hz2[z])) - (hy2[z] - at(hy2, z - 1))
        )
        ey2 = ey[z] - half * ((hx2[z] - at(hx2, z - 1)) - (hz2[z] - xd(hz2[z])))
        ez2 = ez[z] - half * ((hy2[z] - xd(hy2[z])) - (hx2[z] - roll_down(hx2[z])))
        f = [pltpu.roll(fw[c, z], shift, 1)[:, 0:128] for c in range(6)]
        one += ex[z][0:8] * f[0] + ey[z][0:8] * f[1] + ez[z][0:8] * f[2]
        one += hx[z][0:8] * f[3] + hy[z][0:8] * f[4]
        two += ex2[0:8] * f[0] + ey2[0:8] * f[1] + ez2[0:8] * f[2]
        two += hx2[z][0:8] * f[3] + hy2[z][0:8] * f[4] + hz2[z][0:8] * f[5]
        pulse = source_base * (COURANT * fp[z])
        one -= pulse * (w[z][0:8] * c0)
        two -= pulse * (wz[z][0:8] * c0 + w[z][0:8] * c1)
    first, second = jnp.sum(one), jnp.sum(two)
    real = jnp.sum(monitor[0, 0] * shape_zy[...]) + c0 * first + c1 * second
    imaginary = jnp.sum(monitor[0, 1] * shape_zy[...]) - s0 * first - s1 * second
    ids = lanes((8, 128))
    part_out[...] = jnp.where(ids == 0, real, jnp.where(ids == 1, imaginary, 0.0))


def main_kernel(
    strips, grid_rows, ip, fp, ev, od, ff, fs, af, asums, inv_ref, design,
    ev_out, od_out, s_out, p_out,
    field, sums, below, above, hmx, hmz, hmx2, hmz2, ezp, exp, pscr, sem, halo_sem,
):
    strip, source, plane = ip[0], ip[1], ip[2]
    c0, s0, c1, s1 = fp[32], fp[33], fp[34], fp[35]
    copies = []
    for p, f in enumerate((ff, af)):
        copies.append(
            (
                pltpu.make_async_copy(f.at[0, :, 12:24], field.at[p, :, 0:12], sem.at[p, 0]),
                pltpu.make_async_copy(f.at[0, :, 8:12], field.at[p, :, 12:16], sem.at[p, 1]),
            )
        )
    sum_copies = [
        pltpu.make_async_copy(f.at[0], sums.at[p], sem.at[p, 2]) for p, f in enumerate((fs, asums))
    ]
    for p in range(2):
        copies[p][0].start()
        copies[p][1].start()
        sum_copies[p].start()
    from_neighbours(
        ip, ev, od, below, above, pl.ds(16, 2 * UP_ROWS), pl.ds(16, 2 * DOWN_ROWS), halo_sem
    )
    full = (8, NX)
    row_ids = sublanes(full)
    ids = lanes(full)
    first_row, last_row = row_ids == 0, row_ids == 7
    has_below = jnp.where(strip > 0, 1.0, 0.0)
    has_above = jnp.where(strip < strips - 1, 1.0, 0.0)
    base_row = (ROWS * strip).astype(jnp.float32)
    step = 2.0 / grid_rows
    ramp = 1.0 + step * (base_row + row_ids.astype(jnp.float32) + 0.5)
    pulse = jnp.where(ids == source, ramp, 0.0)
    sine_rows = jnp.zeros(full, jnp.float32)
    for k in range(8):
        sine_rows = jnp.where(row_ids == k, fp[SLAB + k], sine_rows)
    sine_rows = jnp.where(ids == source, sine_rows, 0.0)
    ramp_above = 1.0 + step * (base_row + 8.5)
    ramp_below = 1.0 + step * (base_row - 0.5)
    inv_below = inv_ref[15:16]
    inv_above = inv_ref[8:9]

    def y_up(f, halo):
        return jnp.where(last_row, halo, roll_up(f))

    def y_down(f, halo):
        return jnp.where(first_row, halo, roll_down(f))

    for p in range(2):
        up0 = p * UP_ROWS
        down0 = p * DOWN_ROWS
        forward = p == 0

        def get(c, z, p=p):
            return field[p, c, slot(z)]

        def strip_row(c, r, p=p):
            return field[p, c, :, r, :]

        copies[p][0].wait()
        copies[p][1].wait()

        def ex0_above(z):
            k = down0 + z - SLAB if 12 <= z <= 19 else down0 + 32 + {20: 2, 11: 1}[z]
            return above[k : k + 1]

        def ez0_above(z):
            k = down0 + 8 + z - SLAB if 12 <= z <= 19 else down0 + 32 + {20: 0, 11: 7, 10: 6}[z]
            return above[k : k + 1]

        for z in range(10, 21):
            ex, ey, ez = get(0, z), get(1, z), get(2, z)
            hx = get(3, z) - COURANT * ((y_up(ez, ez0_above(z)) - ez) - (get(1, z + 1) - ey))
            hy = get(4, z) - COURANT * ((get(0, z + 1) - ex) - (x_up(ez) - ez))
            field[p, 3, slot(z)] = hx
            field[p, 4, slot(z)] = hy
            if z > 10:
                hz = get(5, z) - COURANT * ((x_up(ey) - ey) - (y_up(ex, ex0_above(z)) - ex))
                field[p, 5, slot(z)] = hz
        dhx = -COURANT * strip_row(2, 0)
        dhz = COURANT * strip_row(0, 0)
        block = [below[up0 + 8 * k : up0 + 8 * k + 8] for k in range(8)]
        extra = block[7]
        hmx[0:8] = has_below * (block[0] + dhx[0:8])
        hmx[8:16] = has_below * (extra + dhx[8:16])
        hmz[0:8] = has_below * (block[1] + dhz[0:8])
        hmz[8:16] = has_below * (pltpu.roll(extra, 6, 0) + dhz[8:16])
        cx = block[4] + dhz[0:8]
        cy = jnp.concatenate([block[5], pltpu.roll(extra, 5, 0)], 0)
        cy = cy + (dhx - roll_down(dhx)) - (dhz - x_down(dhz))
        cz = block[6] - dhx[0:8]
        if forward:
            cz = cz - sine_rows * (c0 * ramp_below)
        both = jnp.concatenate([cy[0:8] * inv_below, cy[8:16]], 0)
        t1 = block[2] + COURANT * ((x_up(both[0:8]) - both[0:8]) + inv_below * cx)
        t2 = block[3] + COURANT * (inv_below * cz + (roll_up(both) - both)[0:8])
        hx7, hz7 = strip_row(3, 7), strip_row(5, 7)
        ab = [above[down0 + 8 * k : down0 + 8 * k + 8] for k in range(5)]
        exp[...] = has_above * (ab[0] + COURANT * inv_above * (ab[2] - hz7[0:8]))
        drive = ab[3] + hx7[0:8]
        if forward:
            drive = drive - sine_rows * (c0 * ramp_above)
        ezp[0:8] = has_above * (ab[1] + COURANT * inv_above * drive)
        drive = ab[4][3:4] + hx7[15:16]
        if forward:
            here = lanes((1, NX)) == source
            drive = drive - jnp.where(here, fp[11] * (c0 * ramp_above), 0.0)
        ezp[15:16] = has_above * (ab[4][7:8] + (COURANT / OXIDE) * drive)
        for z in range(11, 21):
            k = slot(z)
            scale = COURANT * layer_inverse(z, inv_ref[0:8])
            hx, hy, hz = get(3, z), get(4, z), get(5, z)
            ex = get(0, z) + scale * ((hz - y_down(hz, hmz[k : k + 1])) - (hy - get(4, z - 1)))
            ey = get(1, z) + scale * ((hx - get(3, z - 1)) - (hz - x_down(hz)))
            field[p, 0, k] = ex
            field[p, 1, k] = ey
            if z < 20:
                curl = (hy - x_down(hy)) - (hx - y_down(hx, hmx[k : k + 1]))
                if forward:
                    curl = curl - pulse * (fp[z] * c0)
                field[p, 2, k] = get(2, z) + scale * curl
        hmx2[...] = has_below * (hmx[0:8] - COURANT * (strip_row(2, 0)[0:8] - t2))
        hmz2[...] = has_below * (hmz[0:8] - COURANT * (t1 - strip_row(0, 0)[0:8]))
        for z in range(11, 20):
            k = slot(z)
            ex, ey, ez = get(0, z), get(1, z), get(2, z)
            field[p, 3, k] = get(3, z) - COURANT * (
                (y_up(ez, ezp[k : k + 1]) - ez) - (get(1, z + 1) - ey)
            )
            field[p, 4, k] = get(4, z) - COURANT * ((get(0, z + 1) - ex) - (x_up(ez) - ez))
            if z > 11:
                field[p, 5, k] = get(5, z) - COURANT * (
                    (x_up(ey) - ey) - (y_up(ex, exp[k : k + 1]) - ex)
                )
        sum_copies[p].wait()
        scale = COURANT * inv_ref[0:8]
        total = jnp.zeros(full, jnp.float32)
        for z in range(12, 20):
            k = slot(z)
            hx, hy, hz = get(3, z), get(4, z), get(5, z)
            curl_z = (hy - x_down(hy)) - (hx - y_down(hx, hmx2[k : k + 1]))
            if forward:
                curl_z = curl_z - pulse * (fp[z] * c1)
            curls = (
                (hz - y_down(hz, hmz2[k : k + 1])) - (hy - get(4, z - 1)),
                (hx - get(3, z - 1)) - (hz - x_down(hz)),
                curl_z,
            )
            for c in range(3):
                early = get(c, z)
                late = early + scale * curls[c]
                real = sums[p, c, k] + c0 * early + c1 * late
                imaginary = sums[p, 3 + c, k] - s0 * early - s1 * late
                if forward:
                    sums[0, c, k] = real
                    sums[0, 3 + c, k] = imaginary
                else:
                    total = total + (sums[0, c, k] * real - sums[0, 3 + c, k] * imaginary)

    w1 = window_start(plane - 1)
    wide = (16, 256)
    rows_here = cyclic_rows(wide) + ROWS * strip
    valid = (rows_here >= 0) & (rows_here < grid_rows)
    keep = jnp.where(valid, 1.0, 0.0)
    ramps = 1.0 + step * (rows_here.astype(jnp.float32) + 0.5)
    spot = jnp.where(valid & (lanes(wide) + w1 == plane), ramps, 0.0)
    inv_w = inv_ref[:, pl.ds(w1, 256)]
    own_scale = COURANT * inv_w[0:8]
    drive_0 = jnp.zeros((8, 256), jnp.float32)
    drive_1 = jnp.zeros((8, 256), jnp.float32)
    hx_last = hy_last = None
    for z in range(11, 20):
        d1 = spot * layer_inverse(z, inv_w) * (-COURANT * fp[z])
        hy = COURANT * (x_up(d1[0:8]) - d1[0:8])
        hx = keep * (-COURANT * (roll_up(d1) - d1))
        if z > 11:
            k = slot(z)
            e1z = d1[0:8]
            e2x = own_scale * (hy_last - hy)
            e2y = own_scale * (hx - hx_last)[0:8]
            e2z = e1z + own_scale * ((hy - x_down(hy)) - (hx - roll_down(hx))[0:8])
            part = [sums[0, c, k, :, pl.ds(w1, 256)] for c in range(6)]
            drive_0 += (c1 * part[0] + s1 * part[3]) * e2x
            drive_0 += (c1 * part[1] + s1 * part[4]) * e2y
            late = c1 * part[2] + s1 * part[5]
            drive_0 += (c0 * part[2] + s0 * part[5]) * e1z + late * e2z
            drive_1 += late * e1z
        hx_last, hy_last = hx, hy
    design_w = design[:, pl.ds(w1, 256)]
    s_own = total * design[...]
    pscr[:, 0:256] = drive_0 * design_w
    pscr[:, 256:512] = drive_1 * design_w
    pscr[:, 512:1024] = jnp.zeros((8, 512), jnp.float32)
    p_own = pscr[...]
    s_out[...] = s_own
    p_out[...] = p_own
    top = row_ids < 4
    to_up = jnp.where(top, pltpu.roll(s_own, 4, 0), p_own)
    to_down = jnp.where(top, s_own, pltpu.roll(p_own, 4, 0))
    even = strip % 2 == 0
    ev_out[...] = jnp.where(even, to_up, to_down)
    od_out[...] = jnp.where(even, to_down, to_up)


def final_kernel(norm, ip, fp, ev, od, s_own, p_own, totals, keep, send, scr):
    strip, plane, group = ip[0], ip[2], ip[3]
    even = strip % 2 == 0
    low = jnp.where(even, od[...], ev[...])
    high = jnp.where(even, ev[...], od[...])
    both = jnp.concatenate([low[0:4], s_own[...], high[0:4]], 0)
    extra = jnp.concatenate([low[4:8, 0:512], p_own[:, 0:512], high[4:8, 0:512]], 0)
    real = totals[0, 0] / norm
    imaginary = totals[0, 1] / norm
    g0 = real * fp[32] + imaginary * fp[33]
    g1 = real * fp[34] + imaginary * fp[35]
    more = y_smooth(extra, 8)
    w1 = window_start(plane - 1)
    scr[...] = y_smooth(both, 8)
    scr[:, pl.ds(w1, 256)] += g0 * more[:, 0:256] + g1 * more[:, 256:512]
    result = x_smooth(scr[...])
    count = keep.shape[0]
    width = NX // (2 * count)

    def split(mine):
        for k in range(count):
            a = (2 * k + mine) * width
            b = (2 * k + 1 - mine) * width
            keep[k] = result[:, a : a + width]
            send[k] = result[:, b : b + width]

    @pl.when(group % 2 == 0)
    def _():
        split(0)

    @pl.when(group % 2 == 1)
    def _():
        split(1)


def params(limit=VMEM_LIMIT):
    return pltpu.CompilerParams(vmem_limit_bytes=limit)


def swap(value, axis, pairs):
    return lax.ppermute(value, axis, pairs)


def local(
    forward_fields, forward_sums, adjoint_fields, adjoint_sums, monitor_sums, density, labels,
    source_plane, monitor_plane, mode_numbers, frequency, start_phase,
):
    groups = lax.axis_size("exc")
    strips = lax.axis_size("space")
    grid_rows = ROWS * strips
    strip = lax.axis_index("space").astype(jnp.int32)
    group = lax.axis_index("exc").astype(jnp.int32)
    f32 = jnp.float32

    def shaped(*shape):
        return jax.ShapeDtypeStruct(shape, f32)

    even_pairs = [(i, i ^ 1) for i in range(strips)]
    odd_pairs = [(i, ((i - 1) ^ 1) + 1) for i in range(1, strips - 1)]

    ip = jnp.stack([strip, source_plane[0], monitor_plane[0], group])
    layers = jnp.arange(NZ, dtype=f32) + 0.5
    sines = jnp.sin(math.pi * (mode_numbers[0] + 1).astype(f32) * layers / NZ)
    phases = start_phase[0] + frequency[0] * jnp.arange(2, dtype=f32)
    cosines, phase_sines = jnp.cos(phases), jnp.sin(phases)
    factor = frequency[0] * frequency[0] * ((SILICON - OXIDE) / math.sqrt(groups * DZ))
    fp = jnp.concatenate(
        [sines, jnp.stack([cosines[0], phase_sines[0], cosines[1], phase_sines[1], factor])]
    )
    own_rows = (strip * ROWS + jnp.arange(ROWS, dtype=jnp.int32)).astype(f32)
    shape_zy = sines[:, None] * (1.0 + 2.0 * (own_rows + 0.5) / grid_rows)[None, :]

    dens = lax.all_gather(density.T, "exc", axis=1, tiled=True)

    ev, od = pl.pallas_call(
        pack_kernel,
        out_shape=[shaped(PACK, NX), shaped(PACK, NX)],
        in_specs=[SMEM_SPEC, ANY_SPEC, ANY_SPEC, VMEM_SPEC, VMEM_SPEC],
        out_specs=[ANY_SPEC, ANY_SPEC],
        scratch_shapes=[
            pltpu.VMEM((2, 4, 6, 16, NX), f32),
            pltpu.VMEM((PACK, NX), f32),
            pltpu.VMEM((16 + 2 * DOWN_ROWS, NX), f32),
            pltpu.SemaphoreType.DMA((2, 4)),
            pltpu.SemaphoreType.DMA((2,)),
        ],
        compiler_params=params(),
        name="pack",
    )(ip, forward_fields, adjoint_fields, dens, labels)
    ev = swap(ev, "space", even_pairs)
    od = swap(od, "space", odd_pairs)

    def material(*refs):
        material_kernel(grid_rows, *refs)

    inv, design, part = pl.pallas_call(
        material,
        out_shape=[shaped(16, NX), shaped(8, NX), shaped(8, 128)],
        in_specs=[SMEM_SPEC, SMEM_SPEC, ANY_SPEC, ANY_SPEC] + [VMEM_SPEC] * 4 + [ANY_SPEC],
        out_specs=[VMEM_SPEC] * 3,
        scratch_shapes=[
            pltpu.VMEM((16, NX), f32),
            pltpu.VMEM((16, NX), f32),
            pltpu.VMEM((6, NZ, ROWS, 256), f32),
            pltpu.SemaphoreType.DMA((2,)),
            pltpu.SemaphoreType.DMA,
        ],
        compiler_params=params(),
        name="material",
    )(ip, fp, ev, od, dens, labels, monitor_sums, shape_zy, forward_fields)

    totals = part[0:1]
    bit = 1
    while bit < strips:
        totals = totals + swap(totals, "space", [(i, i ^ bit) for i in range(strips)])
        bit *= 2

    def main(*refs):
        main_kernel(strips, grid_rows, *refs)

    ev3, od3, s_own, p_own = pl.pallas_call(
        main,
        out_shape=[shaped(8, NX)] * 4,
        in_specs=[SMEM_SPEC, SMEM_SPEC] + [ANY_SPEC] * 6 + [VMEM_SPEC] * 2,
        out_specs=[VMEM_SPEC] * 4,
        scratch_shapes=[
            pltpu.VMEM((2, 6, 16, ROWS, NX), f32),
            pltpu.VMEM((2, 6, DZ, ROWS, NX), f32),
            pltpu.VMEM((2 * UP_ROWS, NX), f32),
            pltpu.VMEM((2 * DOWN_ROWS, NX), f32),
            pltpu.VMEM((16, NX), f32),
            pltpu.VMEM((16, NX), f32),
            pltpu.VMEM((8, NX), f32),
            pltpu.VMEM((8, NX), f32),
            pltpu.VMEM((16, NX), f32),
            pltpu.VMEM((8, NX), f32),
            pltpu.VMEM((8, NX), f32),
            pltpu.SemaphoreType.DMA((2, 3)),
            pltpu.SemaphoreType.DMA((2,)),
        ],
        compiler_params=params(),
        name="main",
    )(ip, fp, ev, od, forward_fields, forward_sums, adjoint_fields, adjoint_sums, inv, design)
    ev3 = swap(ev3, "space", even_pairs)
    od3 = swap(od3, "space", odd_pairs)

    norm = math.sqrt(NZ * grid_rows)
    half_count = groups // 2

    def final(*refs):
        final_kernel(norm, *refs)

    width = NX // groups
    keep, send = pl.pallas_call(
        final,
        out_shape=[shaped(half_count, ROWS, width)] * 2,
        in_specs=[SMEM_SPEC, SMEM_SPEC] + [VMEM_SPEC] * 4 + [SMEM_SPEC],
        out_specs=[VMEM_SPEC] * 2,
        scratch_shapes=[pltpu.VMEM((8, NX), f32)],
        compiler_params=params(),
        name="final",
    )(ip, fp, ev3, od3, s_own, p_own, totals)
    block = keep + swap(send, "exc", [(i, i ^ 1) for i in range(groups)])
    bit = 2
    while bit < groups:
        count = block.shape[0] // 2
        pairs = block.reshape(count, 2, ROWS, width)
        mine = (group // bit) % 2
        kept = lax.dynamic_index_in_dim(pairs, mine, 1, keepdims=False)
        given = lax.dynamic_index_in_dim(pairs, 1 - mine, 1, keepdims=False)
        block = kept + swap(given, "exc", [(i, i ^ bit) for i in range(groups)])
        bit *= 2
    real, imaginary = totals[0, 0:1] / norm, totals[0, 1:2] / norm
    return block[0].T, real * real + imaginary * imaginary


def solution(mesh):
    in_specs = (
        P("exc", None, None, "space", None),
        P("exc", None, None, "space", None),
        P("exc", None, None, "space", None),
        P("exc", None, None, "space", None),
        P("exc", None, None, "space"),
        P("exc", "space"),
        P("space", None),
        P("exc"),
        P("exc"),
        P("exc"),
        P("exc"),
        P("exc"),
    )
    out_specs = (P("exc", "space"), P("exc"))
    return jax.shard_map(local, mesh=mesh, in_specs=in_specs, out_specs=out_specs, check_vma=False)
```

```python
import math

import jax
import jax.numpy as jnp
from jax import lax
from jax.experimental import pallas as pl
from jax.experimental.pallas import tpu as pltpu
from jax.sharding import PartitionSpec as P

R = 4
COURANT = 0.5
OXIDE = 2.1
SILICON = 12.1
SHARPNESS = 4.0
MIDPOINT = 0.5

ROWS = 8
NX = 1024
NZ = 32
SLAB = 12
DZ = 8
UP_ROWS = 64
DOWN_ROWS = 40
PACK = 2 * UP_ROWS
WEIGHTS = [(R + 1.0 - abs(k - R)) / ((R + 1.0) * (R + 1.0)) for k in range(2 * R + 1)]
VMEM_LIMIT = 50 * 1024 * 1024

SMEM_SPEC = pl.BlockSpec(memory_space=pltpu.SMEM)
VMEM_SPEC = pl.BlockSpec(memory_space=pltpu.VMEM)
ANY_SPEC = pl.BlockSpec(memory_space=pl.ANY)


def slot(z):
    return (z - SLAB) % 16


def lanes(shape):
    return lax.broadcasted_iota(jnp.int32, shape, len(shape) - 1)


def sublanes(shape):
    return lax.broadcasted_iota(jnp.int32, shape, len(shape) - 2)


def x_up(f):
    n = f.shape[-1]
    return jnp.where(lanes(f.shape) == n - 1, 0.0, pltpu.roll(f, n - 1, len(f.shape) - 1))


def x_down(f):
    return jnp.where(lanes(f.shape) == 0, 0.0, pltpu.roll(f, 1, len(f.shape) - 1))


def roll_up(f):
    return pltpu.roll(f, f.shape[0] - 1, 0)


def roll_down(f):
    return pltpu.roll(f, 1, 0)


def y_smooth(f, count):
    total = None
    for k, w in enumerate(WEIGHTS):
        part = w * f[k : k + count]
        total = part if total is None else total + part
    return total


def x_smooth(f):
    n = f.shape[-1]
    ids = lanes(f.shape)
    total = WEIGHTS[R] * f
    for a in range(1, R + 1):
        ahead = jnp.where(ids < n - a, pltpu.roll(f, n - a, 1), 0.0)
        behind = jnp.where(ids >= a, pltpu.roll(f, a, 1), 0.0)
        total = total + WEIGHTS[R + a] * (ahead + behind)
    return total


def pack_kernel(ip, ff, af, ev, od, rows, up, down, sem, out_sem):
    copies = []
    for p, f in enumerate((ff, af)):
        for k, r in enumerate((0, 1, 6, 7)):
            copies.append(pltpu.make_async_copy(f.at[0, :, 8:24, r, :], rows.at[p, k], sem.at[p, k]))
    for c in copies:
        c.start()
    tile = sublanes((8, NX))
    for p in range(2):
        for k in range(4):
            copies[4 * p + k].wait()

        def row(k, c, p=p):
            return pltpu.roll(rows[p, k, c], 12, 0)

        ex, ey, ez = row(0, 0), row(0, 1), row(0, 2)
        ex_n, ez_n = row(1, 0), row(1, 2)
        hx = row(0, 3) - COURANT * ((ez_n - ez) - (roll_up(ey) - ey))
        hy = row(0, 4) - COURANT * ((roll_up(ex) - ex) - (x_up(ez) - ez))
        hz = row(0, 5) - COURANT * ((x_up(ey) - ey) - (ex_n - ex))
        cx = hz - (hy - roll_down(hy))
        cz = (hy - x_down(hy)) - hx
        base = p * DOWN_ROWS
        down[base : base + 8] = ex[0:8]
        down[base + 8 : base + 16] = ez[0:8]
        down[base + 16 : base + 24] = cx[0:8]
        down[base + 24 : base + 32] = cz[0:8]
        extra = jnp.where((tile == 1) | (tile == 2), pltpu.roll(ex[8:16], 2, 0), ez[8:16])
        down[base + 32 : base + 40] = jnp.where(tile == 3, pltpu.roll(cz[8:16], 4, 0), extra)

        ex_l, ey_l, ez_l = row(2, 0), row(2, 1), row(2, 2)
        ex, ey, ez = row(3, 0), row(3, 1), row(3, 2)
        u1 = (x_up(ey) - ey) + ex
        u2 = ez + (roll_up(ey) - ey)
        hx = row(3, 3) + COURANT * u2
        hy = row(3, 4) - COURANT * ((roll_up(ex) - ex) - (x_up(ez) - ez))
        hz = row(3, 5) - COURANT * u1
        hx_l = row(2, 3) - COURANT * ((ez - ez_l) - (roll_up(ey_l) - ey_l))
        hz_l = row(2, 5) - COURANT * ((x_up(ey_l) - ey_l) - (ex - ex_l))
        cx = (hz - hz_l) - (hy - roll_down(hy))
        cy = (hx - roll_down(hx)) - (hz - x_down(hz))
        cz = (hy - x_down(hy)) - (hx - hx_l)
        base = p * UP_ROWS
        for k, v in enumerate((hx, hz, u1, u2, cx, cy, cz)):
            up[base + 8 * k : base + 8 * k + 8] = v[0:8]
        extra = jnp.where((tile == 1) | (tile == 2), pltpu.roll(hz[8:16], 2, 0), hx[8:16])
        up[base + 56 : base + 64] = jnp.where(tile == 3, pltpu.roll(cy[8:16], 3, 0), extra)

    even = ip[0] % 2 == 0

    def send(to_up, to_down):
        a = pltpu.make_async_copy(up, to_up, out_sem.at[0])
        b = pltpu.make_async_copy(down, to_down.at[0 : 2 * DOWN_ROWS], out_sem.at[1])
        a.start()
        b.start()
        a.wait()
        b.wait()

    @pl.when(even)
    def _():
        send(ev, od)

    @pl.when(jnp.logical_not(even))
    def _():
        send(od, ev)


def from_neighbours(ip, ev, od, below, above, below_rows, above_rows, sem):
    even = ip[0] % 2 == 0

    def get(from_below, from_above):
        a = pltpu.make_async_copy(from_below.at[below_rows], below, sem.at[0])
        b = pltpu.make_async_copy(from_above.at[above_rows], above, sem.at[1])
        a.start()
        b.start()
        a.wait()
        b.wait()

    @pl.when(even)
    def _():
        get(od, ev)

    @pl.when(jnp.logical_not(even))
    def _():
        get(ev, od)


def cyclic_rows(shape):
    i = sublanes(shape)
    return jnp.where(i < 12, i, i - 16)


def window_start(first):
    return pl.multiple_of(jnp.clip((first // 128) * 128, 0, NX - 256), 128)


def layer_inverse(z, middle):
    if z < SLAB:
        return 1.0 / OXIDE
    if z >= SLAB + DZ:
        return 1.0
    return middle


def material_kernel(
    grid_rows, ip, fp, ev, od, lab, first, second, third, monitor, shape_zy, ff,
    inv_out, design_out, part_out, wide, fw, win_sem,
):
    strip, plane, group = ip[0], ip[1], ip[3]
    w0 = window_start(plane - 2)
    window = pltpu.make_async_copy(ff.at[0, :, :, :, pl.ds(w0, 256)], fw, win_sem)
    window.start()
    even = strip % 2 == 0
    own = lab[...].astype(jnp.float32)
    low = jnp.where(even, od[4:8, 0:NX], ev[4:8, 0:NX])
    high = jnp.where(even, ev[0:4, 0:NX], od[0:4, 0:NX])
    kinds = jnp.concatenate([low, own, high], 0)
    width = first.shape[1]
    for k in range(4):
        block = (first, second, third, third)[k]
        base = 24 if k == 3 else 0
        at = pl.ds(pl.multiple_of((group ^ k) * width, 128), width)
        mine, from_ev = block[base : base + 8], block[base + 8 : base + 16]
        from_od = block[base + 16 : base + 24]
        wide[0:8, at] = jnp.where(even, from_od, from_ev)
        wide[8:16, at] = mine
        wide[16:24, at] = jnp.where(even, from_ev, from_od)
    filtered = x_smooth(y_smooth(wide[...], 16))
    lower = math.tanh(SHARPNESS * MIDPOINT)
    spread = lower + math.tanh(SHARPNESS * (1.0 - MIDPOINT))
    bent = jnp.tanh(SHARPNESS * (filtered - MIDPOINT))
    projected = (lower + bent) / spread
    steepness = SHARPNESS * (1.0 - bent * bent) / spread
    mixed = OXIDE + (SILICON - OXIDE) * projected
    material = jnp.where(kinds == 2.0, mixed, jnp.where(kinds == 1.0, SILICON, OXIDE))
    inv_out[...] = pltpu.roll(1.0 / material, 12, 0)
    design = jnp.where(kinds == 2.0, steepness * fp[36], 0.0)
    design_out[...] = pltpu.roll(design, 12, 0)[0:8]

    small = (16, 128)
    shift = (64 + w0 - plane + 256) % 256
    middle = pltpu.roll(inv_out[:, pl.ds(w0, 256)], shift, 1)[:, 0:128]
    rows_here = cyclic_rows(small) + ROWS * strip
    xs = lanes(small) + (plane - 64)
    inside = (rows_here >= 0) & (rows_here < grid_rows) & (xs >= 0) & (xs < NX)
    mask = jnp.where(inside, 1.0, 0.0)
    half = COURANT * mask
    ramp = 1.0 + 2.0 * (rows_here.astype(jnp.float32) + 0.5) / grid_rows
    seed_base = jnp.where(lanes(small) == 64, ramp * mask, 0.0)
    source_base = jnp.where(lanes(small) == 64, ramp, 0.0)[0:8]
    zero = jnp.zeros(small, jnp.float32)

    def at(values, z):
        return values[z] if 0 <= z < NZ else zero

    def xu(v):
        return pltpu.roll(v, 127, 1)

    def xd(v):
        return pltpu.roll(v, 1, 1)

    zs = range(NZ)
    inv = [layer_inverse(z, middle) for z in zs]
    seed = [seed_base * fp[z] for z in zs]
    w = [inv[z] * seed[z] for z in zs]
    hx = [half * (roll_up(w[z]) - w[z]) for z in zs]
    hy = [half * (w[z] - xu(w[z])) for z in zs]
    ex = [half * (hy[z] - at(hy, z - 1)) for z in zs]
    ey = [half * (at(hx, z - 1) - hx[z]) for z in zs]
    ez = [
        (seed[z] - COURANT * ((hy[z] - xd(hy[z])) - (hx[z] - roll_down(hx[z])))) * mask for z in zs
    ]
    wx = [inv[z] * ex[z] for z in zs]
    wy = [inv[z] * ey[z] for z in zs]
    wz = [inv[z] * ez[z] for z in zs]
    hx2 = [hx[z] + half * ((roll_up(wz[z]) - wz[z]) - (at(wy, z + 1) - wy[z])) for z in zs]
    hy2 = [hy[z] + half * ((at(wx, z + 1) - wx[z]) - (xu(wz[z]) - wz[z])) for z in zs]
    hz2 = [half * ((xu(wy[z]) - wy[z]) - (roll_up(wx[z]) - wx[z])) for z in zs]
    window.wait()
    one = jnp.zeros((8, 128), jnp.float32)
    two = jnp.zeros((8, 128), jnp.float32)
    c0, s0, c1, s1 = fp[32], fp[33], fp[34], fp[35]
    for z in zs:
        ex2 = ex[z] - half * (
            (hz2[z] - roll_down(hz2[z])) - (hy2[z] - at(hy2, z - 1))
        )
        ey2 = ey[z] - half * ((hx2[z] - at(hx2, z - 1)) - (hz2[z] - xd(hz2[z])))
        ez2 = ez[z] - half * ((hy2[z] - xd(hy2[z])) - (hx2[z] - roll_down(hx2[z])))
        f = [pltpu.roll(fw[c, z], shift, 1)[:, 0:128] for c in range(6)]
        one += ex[z][0:8] * f[0] + ey[z][0:8] * f[1] + ez[z][0:8] * f[2]
        one += hx[z][0:8] * f[3] + hy[z][0:8] * f[4]
        two += ex2[0:8] * f[0] + ey2[0:8] * f[1] + ez2[0:8] * f[2]
        two += hx2[z][0:8] * f[3] + hy2[z][0:8] * f[4] + hz2[z][0:8] * f[5]
        pulse = source_base * (COURANT * fp[z])
        one -= pulse * (w[z][0:8] * c0)
        two -= pulse * (wz[z][0:8] * c0 + w[z][0:8] * c1)
    total_1, total_2 = jnp.sum(one), jnp.sum(two)
    real = jnp.sum(monitor[0, 0] * shape_zy[...]) + c0 * total_1 + c1 * total_2
    imaginary = jnp.sum(monitor[0, 1] * shape_zy[...]) - s0 * total_1 - s1 * total_2
    ids = lanes((8, 128))
    part_out[...] = jnp.where(ids == 0, real, jnp.where(ids == 1, imaginary, 0.0))


def main_kernel(
    strips, grid_rows, ip, fp, ev, od, ff, fs, af, asums, inv_ref, design,
    ev_out, od_out, s_out, p_out,
    field, sums, below, above, hmx, hmz, hmx2, hmz2, ezp, exp, pscr, sem, halo_sem,
):
    strip, source, plane = ip[0], ip[1], ip[2]
    c0, s0, c1, s1 = fp[32], fp[33], fp[34], fp[35]
    copies = []
    for p, f in enumerate((ff, af)):
        copies.append(
            (
                pltpu.make_async_copy(f.at[0, :, 12:24], field.at[p, :, 0:12], sem.at[p, 0]),
                pltpu.make_async_copy(f.at[0, :, 8:12], field.at[p, :, 12:16], sem.at[p, 1]),
            )
        )
    sum_copies = [
        pltpu.make_async_copy(f.at[0], sums.at[p], sem.at[p, 2]) for p, f in enumerate((fs, asums))
    ]
    for p in range(2):
        copies[p][0].start()
        copies[p][1].start()
        sum_copies[p].start()
    from_neighbours(
        ip, ev, od, below, above, pl.ds(0, 2 * UP_ROWS), pl.ds(0, 2 * DOWN_ROWS), halo_sem
    )
    full = (8, NX)
    row_ids = sublanes(full)
    ids = lanes(full)
    first_row, last_row = row_ids == 0, row_ids == 7
    has_below = jnp.where(strip > 0, 1.0, 0.0)
    has_above = jnp.where(strip < strips - 1, 1.0, 0.0)
    base_row = (ROWS * strip).astype(jnp.float32)
    step = 2.0 / grid_rows
    ramp = 1.0 + step * (base_row + row_ids.astype(jnp.float32) + 0.5)
    pulse = jnp.where(ids == source, ramp, 0.0)
    sine_rows = jnp.zeros(full, jnp.float32)
    for k in range(8):
        sine_rows = jnp.where(row_ids == k, fp[SLAB + k], sine_rows)
    sine_rows = jnp.where(ids == source, sine_rows, 0.0)
    ramp_above = 1.0 + step * (base_row + 8.5)
    ramp_below = 1.0 + step * (base_row - 0.5)
    inv_below = inv_ref[15:16]
    inv_above = inv_ref[8:9]

    def y_up(f, halo):
        return jnp.where(last_row, halo, roll_up(f))

    def y_down(f, halo):
        return jnp.where(first_row, halo, roll_down(f))

    for p in range(2):
        up0 = p * UP_ROWS
        down0 = p * DOWN_ROWS
        forward = p == 0

        def get(c, z, p=p):
            return field[p, c, slot(z)]

        def strip_row(c, r, p=p):
            return field[p, c, :, r, :]

        copies[p][0].wait()
        copies[p][1].wait()

        def ex0_above(z):
            k = down0 + z - SLAB if 12 <= z <= 19 else down0 + 32 + {20: 2, 11: 1}[z]
            return above[k : k + 1]

        def ez0_above(z):
            k = down0 + 8 + z - SLAB if 12 <= z <= 19 else down0 + 32 + {20: 0, 11: 7, 10: 6}[z]
            return above[k : k + 1]

        for z in range(10, 21):
            ex, ey, ez = get(0, z), get(1, z), get(2, z)
            hx = get(3, z) - COURANT * ((y_up(ez, ez0_above(z)) - ez) - (get(1, z + 1) - ey))
            hy = get(4, z) - COURANT * ((get(0, z + 1) - ex) - (x_up(ez) - ez))
            field[p, 3, slot(z)] = hx
            field[p, 4, slot(z)] = hy
            if z > 10:
                hz = get(5, z) - COURANT * ((x_up(ey) - ey) - (y_up(ex, ex0_above(z)) - ex))
                field[p, 5, slot(z)] = hz
        dhx = -COURANT * strip_row(2, 0)
        dhz = COURANT * strip_row(0, 0)
        block = [below[up0 + 8 * k : up0 + 8 * k + 8] for k in range(8)]
        extra = block[7]
        hmx[0:8] = has_below * (block[0] + dhx[0:8])
        hmx[8:16] = has_below * (extra + dhx[8:16])
        hmz[0:8] = has_below * (block[1] + dhz[0:8])
        hmz[8:16] = has_below * (pltpu.roll(extra, 6, 0) + dhz[8:16])
        cx = block[4] + dhz[0:8]
        cy = jnp.concatenate([block[5], pltpu.roll(extra, 5, 0)], 0)
        cy = cy + (dhx - roll_down(dhx)) - (dhz - x_down(dhz))
        cz = block[6] - dhx[0:8]
        if forward:
            cz = cz - sine_rows * (c0 * ramp_below)
        both = jnp.concatenate([cy[0:8] * inv_below, cy[8:16]], 0)
        t1 = block[2] + COURANT * ((x_up(both[0:8]) - both[0:8]) + inv_below * cx)
        t2 = block[3] + COURANT * (inv_below * cz + (roll_up(both) - both)[0:8])
        hx7, hz7 = strip_row(3, 7), strip_row(5, 7)
        ab = [above[down0 + 8 * k : down0 + 8 * k + 8] for k in range(5)]
        exp[...] = has_above * (ab[0] + COURANT * inv_above * (ab[2] - hz7[0:8]))
        drive = ab[3] + hx7[0:8]
        if forward:
            drive = drive - sine_rows * (c0 * ramp_above)
        ezp[0:8] = has_above * (ab[1] + COURANT * inv_above * drive)
        drive = ab[4][3:4] + hx7[15:16]
        if forward:
            here = lanes((1, NX)) == source
            drive = drive - jnp.where(here, fp[11] * (c0 * ramp_above), 0.0)
        ezp[15:16] = has_above * (ab[4][7:8] + (COURANT / OXIDE) * drive)
        for z in range(11, 21):
            k = slot(z)
            scale = COURANT * layer_inverse(z, inv_ref[0:8])
            hx, hy, hz = get(3, z), get(4, z), get(5, z)
            ex = get(0, z) + scale * ((hz - y_down(hz, hmz[k : k + 1])) - (hy - get(4, z - 1)))
            ey = get(1, z) + scale * ((hx - get(3, z - 1)) - (hz - x_down(hz)))
            field[p, 0, k] = ex
            field[p, 1, k] = ey
            if z < 20:
                curl = (hy - x_down(hy)) - (hx - y_down(hx, hmx[k : k + 1]))
                if forward:
                    curl = curl - pulse * (fp[z] * c0)
                field[p, 2, k] = get(2, z) + scale * curl
        hmx2[...] = has_below * (hmx[0:8] - COURANT * (strip_row(2, 0)[0:8] - t2))
        hmz2[...] = has_below * (hmz[0:8] - COURANT * (t1 - strip_row(0, 0)[0:8]))
        for z in range(11, 20):
            k = slot(z)
            ex, ey, ez = get(0, z), get(1, z), get(2, z)
            field[p, 3, k] = get(3, z) - COURANT * (
                (y_up(ez, ezp[k : k + 1]) - ez) - (get(1, z + 1) - ey)
            )
            field[p, 4, k] = get(4, z) - COURANT * ((get(0, z + 1) - ex) - (x_up(ez) - ez))
            if z > 11:
                field[p, 5, k] = get(5, z) - COURANT * (
                    (x_up(ey) - ey) - (y_up(ex, exp[k : k + 1]) - ex)
                )
        sum_copies[p].wait()
        scale = COURANT * inv_ref[0:8]
        total = jnp.zeros(full, jnp.float32)
        for z in range(12, 20):
            k = slot(z)
            hx, hy, hz = get(3, z), get(4, z), get(5, z)
            curl_z = (hy - x_down(hy)) - (hx - y_down(hx, hmx2[k : k + 1]))
            if forward:
                curl_z = curl_z - pulse * (fp[z] * c1)
            curls = (
                (hz - y_down(hz, hmz2[k : k + 1])) - (hy - get(4, z - 1)),
                (hx - get(3, z - 1)) - (hz - x_down(hz)),
                curl_z,
            )
            for c in range(3):
                early = get(c, z)
                late = early + scale * curls[c]
                real = sums[p, c, k] + c0 * early + c1 * late
                imaginary = sums[p, 3 + c, k] - s0 * early - s1 * late
                if forward:
                    sums[0, c, k] = real
                    sums[0, 3 + c, k] = imaginary
                else:
                    total = total + (sums[0, c, k] * real - sums[0, 3 + c, k] * imaginary)

    w1 = window_start(plane - 1)
    wide = (16, 256)
    rows_here = cyclic_rows(wide) + ROWS * strip
    valid = (rows_here >= 0) & (rows_here < grid_rows)
    keep = jnp.where(valid, 1.0, 0.0)
    ramps = 1.0 + step * (rows_here.astype(jnp.float32) + 0.5)
    spot = jnp.where(valid & (lanes(wide) + w1 == plane), ramps, 0.0)
    inv_w = inv_ref[:, pl.ds(w1, 256)]
    own_scale = COURANT * inv_w[0:8]
    drive_0 = jnp.zeros((8, 256), jnp.float32)
    drive_1 = jnp.zeros((8, 256), jnp.float32)
    hx_last = hy_last = None
    for z in range(11, 20):
        d1 = spot * layer_inverse(z, inv_w) * (-COURANT * fp[z])
        hy = COURANT * (x_up(d1[0:8]) - d1[0:8])
        hx = keep * (-COURANT * (roll_up(d1) - d1))
        if z > 11:
            k = slot(z)
            e1z = d1[0:8]
            e2x = own_scale * (hy_last - hy)
            e2y = own_scale * (hx - hx_last)[0:8]
            e2z = e1z + own_scale * ((hy - x_down(hy)) - (hx - roll_down(hx))[0:8])
            part = [sums[0, c, k, :, pl.ds(w1, 256)] for c in range(6)]
            drive_0 += (c1 * part[0] + s1 * part[3]) * e2x
            drive_0 += (c1 * part[1] + s1 * part[4]) * e2y
            late = c1 * part[2] + s1 * part[5]
            drive_0 += (c0 * part[2] + s0 * part[5]) * e1z + late * e2z
            drive_1 += late * e1z
        hx_last, hy_last = hx, hy
    design_w = design[:, pl.ds(w1, 256)]
    s_own = total * design[...]
    pscr[:, 0:256] = drive_0 * design_w
    pscr[:, 256:512] = drive_1 * design_w
    pscr[:, 512:1024] = jnp.zeros((8, 512), jnp.float32)
    p_own = pscr[...]
    s_out[...] = s_own
    p_out[...] = p_own
    top = row_ids < 4
    to_up = jnp.where(top, pltpu.roll(s_own, 4, 0), p_own)
    to_down = jnp.where(top, s_own, pltpu.roll(p_own, 4, 0))
    even = strip % 2 == 0
    ev_out[...] = jnp.where(even, to_up, to_down)
    od_out[...] = jnp.where(even, to_down, to_up)


def final_kernel(norm, ip, fp, ev, od, s_own, p_own, totals, keep, send, scr):
    strip, plane, group = ip[0], ip[2], ip[3]
    even = strip % 2 == 0
    low = jnp.where(even, od[...], ev[...])
    high = jnp.where(even, ev[...], od[...])
    both = jnp.concatenate([low[0:4], s_own[...], high[0:4]], 0)
    extra = jnp.concatenate([low[4:8, 0:512], p_own[:, 0:512], high[4:8, 0:512]], 0)
    real = totals[0, 0] / norm
    imaginary = totals[0, 1] / norm
    g0 = real * fp[32] + imaginary * fp[33]
    g1 = real * fp[34] + imaginary * fp[35]
    more = y_smooth(extra, 8)
    w1 = window_start(plane - 1)
    scr[...] = y_smooth(both, 8)
    scr[:, pl.ds(w1, 256)] += g0 * more[:, 0:256] + g1 * more[:, 256:512]
    result = x_smooth(scr[...])
    count = keep.shape[0]
    width = NX // (2 * count)

    def split(mine):
        for k in range(count):
            a = (2 * k + mine) * width
            b = (2 * k + 1 - mine) * width
            keep[k] = result[:, a : a + width]
            send[k] = result[:, b : b + width]

    @pl.when(group % 2 == 0)
    def _():
        split(0)

    @pl.when(group % 2 == 1)
    def _():
        split(1)


def params(limit=VMEM_LIMIT):
    return pltpu.CompilerParams(vmem_limit_bytes=limit)


def swap(value, axis, pairs):
    return lax.ppermute(value, axis, pairs)


def local(
    forward_fields, forward_sums, adjoint_fields, adjoint_sums, monitor_sums, density, labels,
    source_plane, monitor_plane, mode_numbers, frequency, start_phase,
):
    groups = lax.axis_size("exc")
    strips = lax.axis_size("space")
    grid_rows = ROWS * strips
    strip = lax.axis_index("space").astype(jnp.int32)
    group = lax.axis_index("exc").astype(jnp.int32)
    f32 = jnp.float32

    def shaped(*shape):
        return jax.ShapeDtypeStruct(shape, f32)

    even_pairs = [(i, i ^ 1) for i in range(strips)]
    odd_pairs = [(i, ((i - 1) ^ 1) + 1) for i in range(1, strips - 1)]

    ip = jnp.stack([strip, source_plane[0], monitor_plane[0], group])
    number = jnp.arange(128, dtype=jnp.int32)
    order = math.pi * (mode_numbers[0] + 1).astype(f32)
    early = start_phase[0]
    late = start_phase[0] + frequency[0]
    angle = jnp.where(number < 34, early, late)
    angle = jnp.where(number < NZ, order * (number.astype(f32) + 0.5) / NZ, angle)
    fp = jnp.where((number == 32) | (number == 34), jnp.cos(angle), jnp.sin(angle))
    factor = frequency[0] * frequency[0] * ((SILICON - OXIDE) / math.sqrt(groups * DZ))
    fp = jnp.where(number == 36, factor, fp)
    own_rows = (strip * ROWS + jnp.arange(ROWS, dtype=jnp.int32)).astype(f32)
    layers = jnp.arange(NZ, dtype=f32) + 0.5
    ramp = 1.0 + 2.0 * (own_rows + 0.5) / grid_rows
    shape_zy = jnp.sin(order * layers / NZ)[:, None] * ramp[None, :]

    quarter = density.T
    width = quarter.shape[1]
    small = jnp.concatenate([labels.astype(f32), quarter], 1)
    od_small = swap(small, "space", odd_pairs)
    ev_small = swap(small, "space", even_pairs)

    ev, od = pl.pallas_call(
        pack_kernel,
        out_shape=[shaped(PACK, NX), shaped(PACK, NX)],
        in_specs=[SMEM_SPEC, ANY_SPEC, ANY_SPEC],
        out_specs=[ANY_SPEC, ANY_SPEC],
        scratch_shapes=[
            pltpu.VMEM((2, 4, 6, 16, NX), f32),
            pltpu.VMEM((PACK, NX), f32),
            pltpu.VMEM((2 * DOWN_ROWS, NX), f32),
            pltpu.SemaphoreType.DMA((2, 4)),
            pltpu.SemaphoreType.DMA((2,)),
        ],
        compiler_params=params(),
        name="pack",
    )(ip, forward_fields, adjoint_fields)
    od = swap(od, "space", odd_pairs)
    ev = swap(ev, "space", even_pairs)

    first = jnp.concatenate([quarter, ev_small[:, NX:], od_small[:, NX:]], 0)
    second = swap(first, "exc", [(i, i ^ 1) for i in range(groups)])
    third = swap(
        jnp.concatenate([first, second], 0), "exc", [(i, i ^ 2) for i in range(groups)]
    )

    def material(*refs):
        material_kernel(grid_rows, *refs)

    inv, design, part = pl.pallas_call(
        material,
        out_shape=[shaped(16, NX), shaped(8, NX), shaped(8, 128)],
        in_specs=[SMEM_SPEC, SMEM_SPEC] + [VMEM_SPEC] * 8 + [ANY_SPEC],
        out_specs=[VMEM_SPEC] * 3,
        scratch_shapes=[
            pltpu.VMEM((24, NX), f32),
            pltpu.VMEM((6, NZ, ROWS, 256), f32),
            pltpu.SemaphoreType.DMA,
        ],
        compiler_params=params(),
        name="material",
    )(
        ip, fp, ev_small, od_small, labels, first, second, third, monitor_sums, shape_zy,
        forward_fields,
    )

    totals = part[0:1]
    for bit in (8, 24, 4, 1, 3):
        totals = totals + swap(totals, "space", [(i, i ^ bit) for i in range(strips)])

    def main(*refs):
        main_kernel(strips, grid_rows, *refs)

    ev3, od3, s_own, p_own = pl.pallas_call(
        main,
        out_shape=[shaped(8, NX)] * 4,
        in_specs=[SMEM_SPEC, SMEM_SPEC] + [ANY_SPEC] * 6 + [VMEM_SPEC] * 2,
        out_specs=[VMEM_SPEC] * 4,
        scratch_shapes=[
            pltpu.VMEM((2, 6, 16, ROWS, NX), f32),
            pltpu.VMEM((2, 6, DZ, ROWS, NX), f32),
            pltpu.VMEM((2 * UP_ROWS, NX), f32),
            pltpu.VMEM((2 * DOWN_ROWS, NX), f32),
            pltpu.VMEM((16, NX), f32),
            pltpu.VMEM((16, NX), f32),
            pltpu.VMEM((8, NX), f32),
            pltpu.VMEM((8, NX), f32),
            pltpu.VMEM((16, NX), f32),
            pltpu.VMEM((8, NX), f32),
            pltpu.VMEM((8, NX), f32),
            pltpu.SemaphoreType.DMA((2, 3)),
            pltpu.SemaphoreType.DMA((2,)),
        ],
        compiler_params=params(),
        name="main",
    )(ip, fp, ev, od, forward_fields, forward_sums, adjoint_fields, adjoint_sums, inv, design)
    ev3 = swap(ev3, "space", even_pairs)
    od3 = swap(od3, "space", odd_pairs)

    norm = math.sqrt(NZ * grid_rows)
    half_count = groups // 2

    def final(*refs):
        final_kernel(norm, *refs)

    keep, send = pl.pallas_call(
        final,
        out_shape=[shaped(half_count, ROWS, width)] * 2,
        in_specs=[SMEM_SPEC, SMEM_SPEC] + [VMEM_SPEC] * 4 + [SMEM_SPEC],
        out_specs=[VMEM_SPEC] * 2,
        scratch_shapes=[pltpu.VMEM((8, NX), f32)],
        compiler_params=params(),
        name="final",
    )(ip, fp, ev3, od3, s_own, p_own, totals)
    block = keep + swap(send, "exc", [(i, i ^ 1) for i in range(groups)])
    bit = 2
    while bit < groups:
        count = block.shape[0] // 2
        pairs = block.reshape(count, 2, ROWS, width)
        mine = (group // bit) % 2
        kept = lax.dynamic_index_in_dim(pairs, mine, 1, keepdims=False)
        given = lax.dynamic_index_in_dim(pairs, 1 - mine, 1, keepdims=False)
        block = kept + swap(given, "exc", [(i, i ^ bit) for i in range(groups)])
        bit *= 2
    real, imaginary = totals[0, 0:1] / norm, totals[0, 1:2] / norm
    return block[0].T, real * real + imaginary * imaginary


def solution(mesh):
    in_specs = (
        P("exc", None, None, "space", None),
        P("exc", None, None, "space", None),
        P("exc", None, None, "space", None),
        P("exc", None, None, "space", None),
        P("exc", None, None, "space"),
        P("exc", "space"),
        P("space", None),
        P("exc"),
        P("exc"),
        P("exc"),
        P("exc"),
        P("exc"),
    )
    out_specs = (P("exc", "space"), P("exc"))
    return jax.shard_map(local, mesh=mesh, in_specs=in_specs, out_specs=out_specs, check_vma=False)
```

```python
import math

import jax
import jax.numpy as jnp
from jax import lax
from jax.experimental import pallas as pl
from jax.experimental.pallas import tpu as pltpu
from jax.sharding import PartitionSpec as P

R = 4
COURANT = 0.5
OXIDE = 2.1
SILICON = 12.1
SHARPNESS = 4.0
MIDPOINT = 0.5

ROWS = 8
NX = 1024
NZ = 32
SLAB = 12
DZ = 8
UP_ROWS = 64
DOWN_ROWS = 40
PACK = 2 * UP_ROWS
WEIGHTS = [(R + 1.0 - abs(k - R)) / ((R + 1.0) * (R + 1.0)) for k in range(2 * R + 1)]
VMEM_LIMIT = 32 * 1024 * 1024
PACK_LIMIT = 50 * 1024 * 1024

SMEM_SPEC = pl.BlockSpec(memory_space=pltpu.SMEM)
VMEM_SPEC = pl.BlockSpec(memory_space=pltpu.VMEM)
ANY_SPEC = pl.BlockSpec(memory_space=pl.ANY)


def slot(z):
    return (z - SLAB) % 16


def lanes(shape):
    return lax.broadcasted_iota(jnp.int32, shape, len(shape) - 1)


def sublanes(shape):
    return lax.broadcasted_iota(jnp.int32, shape, len(shape) - 2)


def x_up(f):
    n = f.shape[-1]
    return jnp.where(lanes(f.shape) == n - 1, 0.0, pltpu.roll(f, n - 1, len(f.shape) - 1))


def x_down(f):
    return jnp.where(lanes(f.shape) == 0, 0.0, pltpu.roll(f, 1, len(f.shape) - 1))


def roll_up(f):
    return pltpu.roll(f, f.shape[0] - 1, 0)


def roll_down(f):
    return pltpu.roll(f, 1, 0)


def y_smooth(f, count):
    total = None
    for k, w in enumerate(WEIGHTS):
        part = w * f[k : k + count]
        total = part if total is None else total + part
    return total


def x_smooth(f):
    n = f.shape[-1]
    ids = lanes(f.shape)
    total = WEIGHTS[R] * f
    for a in range(1, R + 1):
        ahead = jnp.where(ids < n - a, pltpu.roll(f, n - a, 1), 0.0)
        behind = jnp.where(ids >= a, pltpu.roll(f, a, 1), 0.0)
        total = total + WEIGHTS[R + a] * (ahead + behind)
    return total


def prepare_kernel(grid_rows, scale, mode, rate, phase, fp, shape_yz):
    order = math.pi * (mode[0] + 1).astype(jnp.float32)
    number = lanes((1, 128))
    early, late = phase[0], phase[0] + rate[0]
    angle = jnp.where(number < 34, early, late)
    angle = jnp.where(number < NZ, order * (number.astype(jnp.float32) + 0.5) / NZ, angle)
    value = jnp.where((number == 32) | (number == 34), jnp.cos(angle), jnp.sin(angle))
    fp[...] = jnp.where(number == 36, rate[0] * rate[0] * scale, value)
    small = (ROWS, NZ)
    rows = lax.axis_index("space") * ROWS + sublanes(small)
    ramp = 1.0 + 2.0 * (rows.astype(jnp.float32) + 0.5) / grid_rows
    shape_yz[...] = ramp * jnp.sin(order * (lanes(small).astype(jnp.float32) + 0.5) / NZ)


def pack_kernel(after, ff, af, ev, od, rows, up, down, sem, out_sem):
    copies = []
    for p, f in enumerate((ff, af)):
        for k, r in enumerate((0, 1, 6, 7)):
            copies.append(pltpu.make_async_copy(f.at[0, :, 8:24, r, :], rows.at[p, k], sem.at[p, k]))
    for c in copies:
        c.start()
    tile = sublanes((8, NX))
    for p in range(2):
        for k in range(4):
            copies[4 * p + k].wait()

        def row(k, c, p=p):
            return pltpu.roll(rows[p, k, c], 12, 0)

        ex, ey, ez = row(0, 0), row(0, 1), row(0, 2)
        ex_n, ez_n = row(1, 0), row(1, 2)
        hx = row(0, 3) - COURANT * ((ez_n - ez) - (roll_up(ey) - ey))
        hy = row(0, 4) - COURANT * ((roll_up(ex) - ex) - (x_up(ez) - ez))
        hz = row(0, 5) - COURANT * ((x_up(ey) - ey) - (ex_n - ex))
        cx = hz - (hy - roll_down(hy))
        cz = (hy - x_down(hy)) - hx
        base = p * DOWN_ROWS
        down[base : base + 8] = ex[0:8]
        down[base + 8 : base + 16] = ez[0:8]
        down[base + 16 : base + 24] = cx[0:8]
        down[base + 24 : base + 32] = cz[0:8]
        extra = jnp.where((tile == 1) | (tile == 2), pltpu.roll(ex[8:16], 2, 0), ez[8:16])
        down[base + 32 : base + 40] = jnp.where(tile == 3, pltpu.roll(cz[8:16], 4, 0), extra)

        ex_l, ey_l, ez_l = row(2, 0), row(2, 1), row(2, 2)
        ex, ey, ez = row(3, 0), row(3, 1), row(3, 2)
        u1 = (x_up(ey) - ey) + ex
        u2 = ez + (roll_up(ey) - ey)
        hx = row(3, 3) + COURANT * u2
        hy = row(3, 4) - COURANT * ((roll_up(ex) - ex) - (x_up(ez) - ez))
        hz = row(3, 5) - COURANT * u1
        hx_l = row(2, 3) - COURANT * ((ez - ez_l) - (roll_up(ey_l) - ey_l))
        hz_l = row(2, 5) - COURANT * ((x_up(ey_l) - ey_l) - (ex - ex_l))
        cx = (hz - hz_l) - (hy - roll_down(hy))
        cy = (hx - roll_down(hx)) - (hz - x_down(hz))
        cz = (hy - x_down(hy)) - (hx - hx_l)
        base = p * UP_ROWS
        for k, v in enumerate((hx, hz, u1, u2, cx, cy, cz)):
            up[base + 8 * k : base + 8 * k + 8] = v[0:8]
        extra = jnp.where((tile == 1) | (tile == 2), pltpu.roll(hz[8:16], 2, 0), hx[8:16])
        up[base + 56 : base + 64] = jnp.where(tile == 3, pltpu.roll(cy[8:16], 3, 0), extra)

    even = lax.axis_index("space") % 2 == 0

    def send(to_up, to_down):
        a = pltpu.make_async_copy(up, to_up, out_sem.at[0])
        b = pltpu.make_async_copy(down, to_down.at[0 : 2 * DOWN_ROWS], out_sem.at[1])
        a.start()
        b.start()
        a.wait()
        b.wait()

    @pl.when(even)
    def _():
        send(ev, od)

    @pl.when(jnp.logical_not(even))
    def _():
        send(od, ev)


def stage_kernel(after, ff, af, field, sem):
    copies = []
    for p, f in enumerate((ff, af)):
        copies.append(
            (
                pltpu.make_async_copy(f.at[0, :, 12:22], field.at[p, :, 0:10], sem.at[p, 0]),
                pltpu.make_async_copy(f.at[0, :, 10:12], field.at[p, :, 14:16], sem.at[p, 1]),
            )
        )
    for pair in copies:
        pair[0].start()
        pair[1].start()
    last_row = sublanes((8, NX)) == 7

    def y_up(f):
        return jnp.where(last_row, 0.0, roll_up(f))

    for p in range(2):
        copies[p][0].wait()
        copies[p][1].wait()
        for z in range(10, 21):
            k, n = slot(z), slot(z + 1)
            ex, ey, ez = field[p, 0, k], field[p, 1, k], field[p, 2, k]
            field[p, 3, k] -= COURANT * ((y_up(ez) - ez) - (field[p, 1, n] - ey))
            field[p, 4, k] -= COURANT * ((field[p, 0, n] - ex) - (x_up(ez) - ez))
            if z > 10:
                field[p, 5, k] -= COURANT * ((x_up(ey) - ey) - (y_up(ex) - ex))


def from_neighbours(ev, od, below, above, below_rows, above_rows, sem):
    even = lax.axis_index("space") % 2 == 0

    def get(from_below, from_above):
        a = pltpu.make_async_copy(from_below.at[below_rows], below, sem.at[0])
        b = pltpu.make_async_copy(from_above.at[above_rows], above, sem.at[1])
        a.start()
        b.start()
        a.wait()
        b.wait()

    @pl.when(even)
    def _():
        get(od, ev)

    @pl.when(jnp.logical_not(even))
    def _():
        get(ev, od)


def cyclic_rows(shape):
    i = sublanes(shape)
    return jnp.where(i < 12, i, i - 16)


def window_start(first):
    return pl.multiple_of(jnp.clip((first // 128) * 128, 0, NX - 256), 128)


def layer_inverse(z, middle):
    if z < SLAB:
        return 1.0 / OXIDE
    if z >= SLAB + DZ:
        return 1.0
    return middle


def material_kernel(
    grid_rows, source_at, fp, ev, od, own, monitor, shape_yz, ff,
    inv_out, design_out, part_out, wide, fw, win_sem,
):
    strip, group = lax.axis_index("space"), lax.axis_index("exc")
    plane = source_at[0]
    w0 = window_start(plane - 2)
    window = pltpu.make_async_copy(ff.at[0, :, :, :, pl.ds(w0, 256)], fw, win_sem)
    window.start()
    even = strip % 2 == 0
    both = jnp.concatenate(
        [jnp.where(even, od[...], ev[...]), own[...], jnp.where(even, ev[...], od[...])], 0
    )
    kinds = both[4:20, NX:]
    for k in range(4):
        at = pl.ds(pl.multiple_of((group ^ k) * 256, 128), 256)
        wide[:, at] = both[:, 256 * k : 256 * k + 256]
    filtered = x_smooth(y_smooth(wide[...], 16))
    lower = math.tanh(SHARPNESS * MIDPOINT)
    spread = lower + math.tanh(SHARPNESS * (1.0 - MIDPOINT))
    bent = jnp.tanh(SHARPNESS * (filtered - MIDPOINT))
    projected = (lower + bent) / spread
    steepness = SHARPNESS * (1.0 - bent * bent) / spread
    mixed = OXIDE + (SILICON - OXIDE) * projected
    material = jnp.where(kinds == 2.0, mixed, jnp.where(kinds == 1.0, SILICON, OXIDE))
    inv_out[...] = pltpu.roll(1.0 / material, 12, 0)
    design = jnp.where(kinds == 2.0, steepness * fp[0, 36], 0.0)
    design_out[...] = pltpu.roll(design, 12, 0)[0:8]

    small = (16, 128)
    shift = (64 + w0 - plane + 256) % 256
    middle = pltpu.roll(inv_out[:, pl.ds(w0, 256)], shift, 1)[:, 0:128]
    rows_here = cyclic_rows(small) + ROWS * strip
    xs = lanes(small) + (plane - 64)
    inside = (rows_here >= 0) & (rows_here < grid_rows) & (xs >= 0) & (xs < NX)
    mask = jnp.where(inside, 1.0, 0.0)
    half = COURANT * mask
    ramp = 1.0 + 2.0 * (rows_here.astype(jnp.float32) + 0.5) / grid_rows
    seed_base = jnp.where(lanes(small) == 64, ramp * mask, 0.0)
    source_base = jnp.where(lanes(small) == 64, ramp, 0.0)[0:8]
    zero = jnp.zeros(small, jnp.float32)

    def at(values, z):
        return values[z] if 0 <= z < NZ else zero

    def xu(v):
        return pltpu.roll(v, 127, 1)

    def xd(v):
        return pltpu.roll(v, 1, 1)

    zs = range(NZ)
    inv = [layer_inverse(z, middle) for z in zs]
    seed = [seed_base * fp[0, z] for z in zs]
    w = [inv[z] * seed[z] for z in zs]
    hx = [half * (roll_up(w[z]) - w[z]) for z in zs]
    hy = [half * (w[z] - xu(w[z])) for z in zs]
    ex = [half * (hy[z] - at(hy, z - 1)) for z in zs]
    ey = [half * (at(hx, z - 1) - hx[z]) for z in zs]
    ez = [
        (seed[z] - COURANT * ((hy[z] - xd(hy[z])) - (hx[z] - roll_down(hx[z])))) * mask for z in zs
    ]
    wx = [inv[z] * ex[z] for z in zs]
    wy = [inv[z] * ey[z] for z in zs]
    wz = [inv[z] * ez[z] for z in zs]
    hx2 = [hx[z] + half * ((roll_up(wz[z]) - wz[z]) - (at(wy, z + 1) - wy[z])) for z in zs]
    hy2 = [hy[z] + half * ((at(wx, z + 1) - wx[z]) - (xu(wz[z]) - wz[z])) for z in zs]
    hz2 = [half * ((xu(wy[z]) - wy[z]) - (roll_up(wx[z]) - wx[z])) for z in zs]
    window.wait()
    one = jnp.zeros((8, 128), jnp.float32)
    two = jnp.zeros((8, 128), jnp.float32)
    c0, s0, c1, s1 = fp[0, 32], fp[0, 33], fp[0, 34], fp[0, 35]
    for z in zs:
        ex2 = ex[z] - half * (
            (hz2[z] - roll_down(hz2[z])) - (hy2[z] - at(hy2, z - 1))
        )
        ey2 = ey[z] - half * ((hx2[z] - at(hx2, z - 1)) - (hz2[z] - xd(hz2[z])))
        ez2 = ez[z] - half * ((hy2[z] - xd(hy2[z])) - (hx2[z] - roll_down(hx2[z])))
        f = [pltpu.roll(fw[c, z], shift, 1)[:, 0:128] for c in range(6)]
        one += ex[z][0:8] * f[0] + ey[z][0:8] * f[1] + ez[z][0:8] * f[2]
        one += hx[z][0:8] * f[3] + hy[z][0:8] * f[4]
        two += ex2[0:8] * f[0] + ey2[0:8] * f[1] + ez2[0:8] * f[2]
        two += hx2[z][0:8] * f[3] + hy2[z][0:8] * f[4] + hz2[z][0:8] * f[5]
        pulse = source_base * (COURANT * fp[0, z])
        one -= pulse * (w[z][0:8] * c0)
        two -= pulse * (wz[z][0:8] * c0 + w[z][0:8] * c1)
    total_1, total_2 = jnp.sum(one), jnp.sum(two)
    real = jnp.sum(monitor[0, 0] * shape_yz[...]) + c0 * total_1 + c1 * total_2
    imaginary = jnp.sum(monitor[0, 1] * shape_yz[...]) - s0 * total_1 - s1 * total_2
    ids = lanes((8, 128))
    part_out[...] = jnp.where(ids == 0, real, jnp.where(ids == 1, imaginary, 0.0))


def main_kernel(
    strips, grid_rows, source_at, monitor_at, fp, ev, od, staged, fs, asums, inv_ref, design,
    ev_out, od_out, s_out, p_out,
    field, sums, below, above, hmx, hmz, hmx2, hmz2, ezp, exp, pscr, sem, halo_sem,
):
    strip = lax.axis_index("space")
    source, plane = source_at[0], monitor_at[0]
    c0, s0, c1, s1 = fp[0, 32], fp[0, 33], fp[0, 34], fp[0, 35]
    sum_copies = [
        pltpu.make_async_copy(f.at[0], sums.at[p], sem.at[p, 2]) for p, f in enumerate((fs, asums))
    ]
    for p in range(2):
        sum_copies[p].start()
    from_neighbours(
        ev, od, below, above, pl.ds(0, 2 * UP_ROWS), pl.ds(0, 2 * DOWN_ROWS), halo_sem
    )
    full = (8, NX)
    row_ids = sublanes(full)
    ids = lanes(full)
    first_row, last_row = row_ids == 0, row_ids == 7
    has_below = jnp.where(strip > 0, 1.0, 0.0)
    has_above = jnp.where(strip < strips - 1, 1.0, 0.0)
    base_row = (ROWS * strip).astype(jnp.float32)
    step = 2.0 / grid_rows
    ramp = 1.0 + step * (base_row + row_ids.astype(jnp.float32) + 0.5)
    pulse = jnp.where(ids == source, ramp, 0.0)
    sine_rows = jnp.zeros(full, jnp.float32)
    for k in range(8):
        sine_rows = jnp.where(row_ids == k, fp[0, SLAB + k], sine_rows)
    sine_rows = jnp.where(ids == source, sine_rows, 0.0)
    ramp_above = 1.0 + step * (base_row + 8.5)
    ramp_below = 1.0 + step * (base_row - 0.5)
    inv_below = inv_ref[15:16]
    inv_above = inv_ref[8:9]

    def y_up(f, halo):
        return jnp.where(last_row, halo, roll_up(f))

    def y_down(f, halo):
        return jnp.where(first_row, halo, roll_down(f))

    for p in range(2):
        up0 = p * UP_ROWS
        down0 = p * DOWN_ROWS
        forward = p == 0

        def get(c, z, p=p):
            return field[p, c, slot(z)]

        def strip_row(c, r, p=p):
            return field[p, c, :, r, :]

        def start(c, z, p=p):
            return staged[p, c, slot(z)]

        def ex0_above(z):
            k = down0 + z - SLAB if 12 <= z <= 19 else down0 + 32 + {20: 2, 11: 1}[z]
            return above[k : k + 1]

        def ez0_above(z):
            k = down0 + 8 + z - SLAB if 12 <= z <= 19 else down0 + 32 + {20: 0, 11: 7, 10: 6}[z]
            return above[k : k + 1]

        for z in range(10, 21):
            k = slot(z)
            field[p, 3, k] = start(3, z) - jnp.where(last_row, COURANT * ez0_above(z), 0.0)
            if z > 10:
                field[p, 5, k] = start(5, z) + jnp.where(last_row, COURANT * ex0_above(z), 0.0)
        dhx = -COURANT * staged[p, 2, :, 0, :]
        dhz = COURANT * staged[p, 0, :, 0, :]
        block = [below[up0 + 8 * k : up0 + 8 * k + 8] for k in range(8)]
        extra = block[7]
        hmx[0:8] = has_below * (block[0] + dhx[0:8])
        hmx[8:16] = has_below * (extra + dhx[8:16])
        hmz[0:8] = has_below * (block[1] + dhz[0:8])
        hmz[8:16] = has_below * (pltpu.roll(extra, 6, 0) + dhz[8:16])
        cx = block[4] + dhz[0:8]
        cy = jnp.concatenate([block[5], pltpu.roll(extra, 5, 0)], 0)
        cy = cy + (dhx - roll_down(dhx)) - (dhz - x_down(dhz))
        cz = block[6] - dhx[0:8]
        if forward:
            cz = cz - sine_rows * (c0 * ramp_below)
        both = jnp.concatenate([cy[0:8] * inv_below, cy[8:16]], 0)
        t1 = block[2] + COURANT * ((x_up(both[0:8]) - both[0:8]) + inv_below * cx)
        t2 = block[3] + COURANT * (inv_below * cz + (roll_up(both) - both)[0:8])
        hx7, hz7 = strip_row(3, 7), strip_row(5, 7)
        ab = [above[down0 + 8 * k : down0 + 8 * k + 8] for k in range(5)]
        exp[...] = has_above * (ab[0] + COURANT * inv_above * (ab[2] - hz7[0:8]))
        drive = ab[3] + hx7[0:8]
        if forward:
            drive = drive - sine_rows * (c0 * ramp_above)
        ezp[0:8] = has_above * (ab[1] + COURANT * inv_above * drive)
        drive = ab[4][3:4] + hx7[15:16]
        if forward:
            here = lanes((1, NX)) == source
            drive = drive - jnp.where(here, fp[0, 11] * (c0 * ramp_above), 0.0)
        ezp[15:16] = has_above * (ab[4][7:8] + (COURANT / OXIDE) * drive)
        for z in range(11, 21):
            k = slot(z)
            scale = COURANT * layer_inverse(z, inv_ref[0:8])
            hx, hy, hz = get(3, z), start(4, z), get(5, z)
            ex = start(0, z) + scale * ((hz - y_down(hz, hmz[k : k + 1])) - (hy - start(4, z - 1)))
            ey = start(1, z) + scale * ((hx - get(3, z - 1)) - (hz - x_down(hz)))
            field[p, 0, k] = ex
            field[p, 1, k] = ey
            if z < 20:
                curl = (hy - x_down(hy)) - (hx - y_down(hx, hmx[k : k + 1]))
                if forward:
                    curl = curl - pulse * (fp[0, z] * c0)
                field[p, 2, k] = start(2, z) + scale * curl
        hmx2[...] = has_below * (hmx[0:8] - COURANT * (strip_row(2, 0)[0:8] - t2))
        hmz2[...] = has_below * (hmz[0:8] - COURANT * (t1 - strip_row(0, 0)[0:8]))
        for z in range(11, 20):
            k = slot(z)
            ex, ey, ez = get(0, z), get(1, z), get(2, z)
            field[p, 3, k] = get(3, z) - COURANT * (
                (y_up(ez, ezp[k : k + 1]) - ez) - (get(1, z + 1) - ey)
            )
            field[p, 4, k] = start(4, z) - COURANT * ((get(0, z + 1) - ex) - (x_up(ez) - ez))
            if z > 11:
                field[p, 5, k] = get(5, z) - COURANT * (
                    (x_up(ey) - ey) - (y_up(ex, exp[k : k + 1]) - ex)
                )
        sum_copies[p].wait()
        scale = COURANT * inv_ref[0:8]
        total = jnp.zeros(full, jnp.float32)
        for z in range(12, 20):
            k = slot(z)
            hx, hy, hz = get(3, z), get(4, z), get(5, z)
            curl_z = (hy - x_down(hy)) - (hx - y_down(hx, hmx2[k : k + 1]))
            if forward:
                curl_z = curl_z - pulse * (fp[0, z] * c1)
            curls = (
                (hz - y_down(hz, hmz2[k : k + 1])) - (hy - get(4, z - 1)),
                (hx - get(3, z - 1)) - (hz - x_down(hz)),
                curl_z,
            )
            for c in range(3):
                early = get(c, z)
                late = early + scale * curls[c]
                real = sums[p, c, k] + c0 * early + c1 * late
                imaginary = sums[p, 3 + c, k] - s0 * early - s1 * late
                if forward:
                    sums[0, c, k] = real
                    sums[0, 3 + c, k] = imaginary
                else:
                    total = total + (sums[0, c, k] * real - sums[0, 3 + c, k] * imaginary)

    w1 = window_start(plane - 1)
    wide = (16, 256)
    rows_here = cyclic_rows(wide) + ROWS * strip
    valid = (rows_here >= 0) & (rows_here < grid_rows)
    keep = jnp.where(valid, 1.0, 0.0)
    ramps = 1.0 + step * (rows_here.astype(jnp.float32) + 0.5)
    spot = jnp.where(valid & (lanes(wide) + w1 == plane), ramps, 0.0)
    inv_w = inv_ref[:, pl.ds(w1, 256)]
    own_scale = COURANT * inv_w[0:8]
    drive_0 = jnp.zeros((8, 256), jnp.float32)
    drive_1 = jnp.zeros((8, 256), jnp.float32)
    hx_last = hy_last = None
    for z in range(11, 20):
        d1 = spot * layer_inverse(z, inv_w) * (-COURANT * fp[0, z])
        hy = COURANT * (x_up(d1[0:8]) - d1[0:8])
        hx = keep * (-COURANT * (roll_up(d1) - d1))
        if z > 11:
            k = slot(z)
            e1z = d1[0:8]
            e2x = own_scale * (hy_last - hy)
            e2y = own_scale * (hx - hx_last)[0:8]
            e2z = e1z + own_scale * ((hy - x_down(hy)) - (hx - roll_down(hx))[0:8])
            part = [sums[0, c, k, :, pl.ds(w1, 256)] for c in range(6)]
            drive_0 += (c1 * part[0] + s1 * part[3]) * e2x
            drive_0 += (c1 * part[1] + s1 * part[4]) * e2y
            late = c1 * part[2] + s1 * part[5]
            drive_0 += (c0 * part[2] + s0 * part[5]) * e1z + late * e2z
            drive_1 += late * e1z
        hx_last, hy_last = hx, hy
    design_w = design[:, pl.ds(w1, 256)]
    s_own = total * design[...]
    pscr[:, 0:256] = drive_0 * design_w
    pscr[:, 256:512] = drive_1 * design_w
    pscr[:, 512:1024] = jnp.zeros((8, 512), jnp.float32)
    p_own = pscr[...]
    s_out[...] = s_own
    p_out[...] = p_own
    top = row_ids < 4
    to_up = jnp.where(top, pltpu.roll(s_own, 4, 0), p_own)
    to_down = jnp.where(top, s_own, pltpu.roll(p_own, 4, 0))
    even = strip % 2 == 0
    ev_out[...] = jnp.where(even, to_up, to_down)
    od_out[...] = jnp.where(even, to_down, to_up)


def final_kernel(norm, monitor_at, fp, ev, od, s_own, p_own, totals, keep, send, merit, scr):
    strip, group = lax.axis_index("space"), lax.axis_index("exc")
    plane = monitor_at[0]
    even = strip % 2 == 0
    low = jnp.where(even, od[...], ev[...])
    high = jnp.where(even, ev[...], od[...])
    sums = totals[...] + ev[4:5, 512:640]
    ids = lanes((1, 128))
    real = jnp.sum(jnp.where(ids == 0, sums, 0.0), axis=1, keepdims=True) / norm
    imaginary = jnp.sum(jnp.where(ids == 1, sums, 0.0), axis=1, keepdims=True) / norm
    both = jnp.concatenate([low[0:4], s_own[...], high[0:4]], 0)
    extra = jnp.concatenate([low[4:8, 0:512], p_own[:, 0:512], high[4:8, 0:512]], 0)
    merit[...] = jnp.broadcast_to(real * real + imaginary * imaginary, (1, 128))
    g0 = real * fp[0, 32] + imaginary * fp[0, 33]
    g1 = real * fp[0, 34] + imaginary * fp[0, 35]
    more = y_smooth(extra, 8)
    w1 = window_start(plane - 1)
    scr[...] = y_smooth(both, 8)
    scr[:, pl.ds(w1, 256)] += g0 * more[:, 0:256] + g1 * more[:, 256:512]
    result = x_smooth(scr[...])
    count = keep.shape[0]
    width = NX // (2 * count)

    def split(mine):
        for k in range(count):
            a = (2 * k + mine) * width
            b = (2 * k + 1 - mine) * width
            keep[k] = result[:, a : a + width]
            send[k] = result[:, b : b + width]

    @pl.when(group % 2 == 0)
    def _():
        split(0)

    @pl.when(group % 2 == 1)
    def _():
        split(1)


def params(limit=VMEM_LIMIT):
    return pltpu.CompilerParams(vmem_limit_bytes=limit)


def swap(value, axis, pairs):
    return lax.ppermute(value, axis, pairs)


def local(
    forward_fields, forward_sums, adjoint_fields, adjoint_sums, monitor_sums, density, labels,
    source_plane, monitor_plane, mode_numbers, frequency, start_phase,
):
    groups = lax.axis_size("exc")
    strips = lax.axis_size("space")
    grid_rows = ROWS * strips
    group = lax.axis_index("exc").astype(jnp.int32)
    f32 = jnp.float32

    def shaped(*shape):
        return jax.ShapeDtypeStruct(shape, f32)

    even_pairs = [(i, i ^ 1) for i in range(strips)]
    odd_pairs = [(i, ((i - 1) ^ 1) + 1) for i in range(1, strips - 1)]

    fp, shape_yz = pl.pallas_call(
        lambda *refs: prepare_kernel(grid_rows, (SILICON - OXIDE) / math.sqrt(groups * DZ), *refs),
        out_shape=[shaped(1, 128), shaped(ROWS, NZ)],
        in_specs=[SMEM_SPEC] * 3,
        out_specs=[VMEM_SPEC] * 2,
        name="prepare",
    )(mode_numbers, frequency, start_phase)

    quarter = density.T
    width = quarter.shape[1]
    second = swap(quarter, "exc", [(i, i ^ 1) for i in range(groups)])
    third = swap(
        jnp.concatenate([quarter, second], 0), "exc", [(i, i ^ 2) for i in range(groups)]
    )
    small = jnp.concatenate(
        [quarter, second, third[0:8], third[8:16], labels.astype(f32)], 1
    )
    od_small = swap(small, "space", odd_pairs)
    ev_small = swap(small, "space", even_pairs)

    ev, od = pl.pallas_call(
        pack_kernel,
        out_shape=[shaped(PACK, NX), shaped(PACK, NX)],
        in_specs=[ANY_SPEC] * 3,
        out_specs=[ANY_SPEC, ANY_SPEC],
        scratch_shapes=[
            pltpu.VMEM((2, 4, 6, 16, NX), f32),
            pltpu.VMEM((PACK, NX), f32),
            pltpu.VMEM((2 * DOWN_ROWS, NX), f32),
            pltpu.SemaphoreType.DMA((2, 4)),
            pltpu.SemaphoreType.DMA((2,)),
        ],
        compiler_params=params(PACK_LIMIT),
        name="pack",
    )(second, forward_fields, adjoint_fields)
    staged = pl.pallas_call(
        stage_kernel,
        out_shape=shaped(2, 6, 16, ROWS, NX),
        in_specs=[ANY_SPEC] * 3,
        out_specs=VMEM_SPEC,
        scratch_shapes=[pltpu.SemaphoreType.DMA((2, 2))],
        compiler_params=params(PACK_LIMIT),
        name="stage",
    )(small, forward_fields, adjoint_fields)
    od = swap(od, "space", odd_pairs)
    ev = swap(ev, "space", even_pairs)

    fp, staged = lax.optimization_barrier((fp, staged))

    def material(*refs):
        material_kernel(grid_rows, *refs)

    inv, design, part = pl.pallas_call(
        material,
        out_shape=[shaped(16, NX), shaped(8, NX), shaped(8, 128)],
        in_specs=[SMEM_SPEC, SMEM_SPEC] + [VMEM_SPEC] * 5 + [ANY_SPEC],
        out_specs=[VMEM_SPEC] * 3,
        scratch_shapes=[
            pltpu.VMEM((24, NX), f32),
            pltpu.VMEM((6, NZ, ROWS, 256), f32),
            pltpu.SemaphoreType.DMA,
        ],
        compiler_params=params(),
        name="material",
    )(
        source_plane, fp, ev_small, od_small, small, monitor_sums.transpose(0, 1, 3, 2), shape_yz,
        forward_fields,
    )

    totals = part[0:1]

    def fold(totals, bit):
        return totals + swap(totals, "space", [(i, i ^ bit) for i in range(strips)])

    arriving = swap(totals, "space", [(i, i ^ 4) for i in range(strips)])
    def main(*refs):
        main_kernel(strips, grid_rows, *refs)

    ev3, od3, s_own, p_own = pl.pallas_call(
        main,
        out_shape=[shaped(8, NX)] * 4,
        in_specs=[SMEM_SPEC] * 3 + [ANY_SPEC] * 2 + [VMEM_SPEC] + [ANY_SPEC] * 2 + [VMEM_SPEC] * 2,
        out_specs=[VMEM_SPEC] * 4,
        scratch_shapes=[
            pltpu.VMEM((2, 6, 16, ROWS, NX), f32),
            pltpu.VMEM((2, 6, DZ, ROWS, NX), f32),
            pltpu.VMEM((2 * UP_ROWS, NX), f32),
            pltpu.VMEM((2 * DOWN_ROWS, NX), f32),
            pltpu.VMEM((16, NX), f32),
            pltpu.VMEM((16, NX), f32),
            pltpu.VMEM((8, NX), f32),
            pltpu.VMEM((8, NX), f32),
            pltpu.VMEM((16, NX), f32),
            pltpu.VMEM((8, NX), f32),
            pltpu.VMEM((8, NX), f32),
            pltpu.SemaphoreType.DMA((2, 3)),
            pltpu.SemaphoreType.DMA((2,)),
        ],
        compiler_params=params(),
        name="main",
    )(
        source_plane, monitor_plane, fp, ev, od, staged, forward_sums, adjoint_sums, inv, design,
    )
    od3, totals = lax.optimization_barrier((od3, totals))
    totals = totals + arriving
    od3 = swap(od3, "space", odd_pairs)
    totals = fold(totals, 8)
    totals = fold(totals, 24)
    totals = fold(totals, 3)
    ev3 = swap(lax.dynamic_update_slice(ev3, totals, (4, 512)), "space", even_pairs)

    norm = math.sqrt(NZ * grid_rows)
    half_count = groups // 2

    def final(*refs):
        final_kernel(norm, *refs)

    keep, send, merit = pl.pallas_call(
        final,
        out_shape=[shaped(half_count, ROWS, width)] * 2 + [shaped(1, 128)],
        in_specs=[SMEM_SPEC, SMEM_SPEC] + [VMEM_SPEC] * 5,
        out_specs=[VMEM_SPEC] * 3,
        scratch_shapes=[pltpu.VMEM((8, NX), f32)],
        compiler_params=params(),
        name="final",
    )(monitor_plane, fp, ev3, od3, s_own, p_own, totals)
    block = keep + swap(send, "exc", [(i, i ^ 1) for i in range(groups)])
    bit = 2
    while bit < groups:
        count = block.shape[0] // 2
        pairs = block.reshape(count, 2, ROWS, width)
        mine = (group // bit) % 2
        kept = lax.dynamic_index_in_dim(pairs, mine, 1, keepdims=False)
        given = lax.dynamic_index_in_dim(pairs, 1 - mine, 1, keepdims=False)
        block = kept + swap(given, "exc", [(i, i ^ bit) for i in range(groups)])
        bit *= 2
    return block[0].T, merit[0, 0:1]


def solution(mesh):
    in_specs = (
        P("exc", None, None, "space", None),
        P("exc", None, None, "space", None),
        P("exc", None, None, "space", None),
        P("exc", None, None, "space", None),
        P("exc", None, None, "space"),
        P("exc", "space"),
        P("space", None),
        P("exc"),
        P("exc"),
        P("exc"),
        P("exc"),
        P("exc"),
    )
    out_specs = (P("exc", "space"), P("exc"))
    return jax.shard_map(local, mesh=mesh, in_specs=in_specs, out_specs=out_specs, check_vma=False)
```

```python
import math

import jax
import jax.numpy as jnp
from jax import lax
from jax.experimental import pallas as pl
from jax.experimental.pallas import tpu as pltpu
from jax.sharding import PartitionSpec as P

R = 4
COURANT = 0.5
OXIDE = 2.1
SILICON = 12.1
SHARPNESS = 4.0
MIDPOINT = 0.5

ROWS = 8
NX = 1024
NZ = 32
SLAB = 12
DZ = 8
UP_ROWS = 64
DOWN_ROWS = 40
PACK = 2 * UP_ROWS
WEIGHTS = [(R + 1.0 - abs(k - R)) / ((R + 1.0) * (R + 1.0)) for k in range(2 * R + 1)]
VMEM_LIMIT = 32 * 1024 * 1024
PACK_LIMIT = 50 * 1024 * 1024

SMEM_SPEC = pl.BlockSpec(memory_space=pltpu.SMEM)
VMEM_SPEC = pl.BlockSpec(memory_space=pltpu.VMEM)
ANY_SPEC = pl.BlockSpec(memory_space=pl.ANY)


def slot(z):
    return (z - SLAB) % 16


def lanes(shape):
    return lax.broadcasted_iota(jnp.int32, shape, len(shape) - 1)


def sublanes(shape):
    return lax.broadcasted_iota(jnp.int32, shape, len(shape) - 2)


def x_up(f):
    n = f.shape[-1]
    return jnp.where(lanes(f.shape) == n - 1, 0.0, pltpu.roll(f, n - 1, len(f.shape) - 1))


def x_down(f):
    return jnp.where(lanes(f.shape) == 0, 0.0, pltpu.roll(f, 1, len(f.shape) - 1))


def roll_up(f):
    return pltpu.roll(f, f.shape[0] - 1, 0)


def roll_down(f):
    return pltpu.roll(f, 1, 0)


def y_smooth(f, count):
    total = None
    for k, w in enumerate(WEIGHTS):
        part = w * f[k : k + count]
        total = part if total is None else total + part
    return total


def x_smooth(f):
    n = f.shape[-1]
    ids = lanes(f.shape)
    total = WEIGHTS[R] * f
    for a in range(1, R + 1):
        ahead = jnp.where(ids < n - a, pltpu.roll(f, n - a, 1), 0.0)
        behind = jnp.where(ids >= a, pltpu.roll(f, a, 1), 0.0)
        total = total + WEIGHTS[R + a] * (ahead + behind)
    return total


def prepare_kernel(grid_rows, scale, mode_at, rate_at, phase_at, source_at, monitor_at, fp, shape_yz):
    order = math.pi * (mode_at[...] + 1).astype(jnp.float32)
    rate, phase = rate_at[...], phase_at[...]
    number = lanes((1, 128))
    early, late = phase, phase + rate
    angle = jnp.where(number < 34, early, late)
    angle = jnp.where(number < NZ, order * (number.astype(jnp.float32) + 0.5) / NZ, angle)
    value = jnp.where((number == 32) | (number == 34), jnp.cos(angle), jnp.sin(angle))
    value = jnp.where(number == 36, rate * rate * scale, value)
    value = jnp.where(number == 37, source_at[...].astype(jnp.float32), value)
    fp[...] = jnp.where(number == 38, monitor_at[...].astype(jnp.float32), value)
    small = (ROWS, NZ)
    rows = lax.axis_index("space") * ROWS + sublanes(small)
    ramp = 1.0 + 2.0 * (rows.astype(jnp.float32) + 0.5) / grid_rows
    shape_yz[...] = ramp * jnp.sin(order * (lanes(small).astype(jnp.float32) + 0.5) / NZ)


def pack_kernel(even_goes_up, after, ff, af, out, rows, sem):
    tile = sublanes((8, NX))
    even = lax.axis_index("space") % 2 == 0
    goes_up = even if even_goes_up else jnp.logical_not(even)

    def load(first):
        copies = []
        for p, f in enumerate((ff, af)):
            for k in range(2):
                copies.append(
                    pltpu.make_async_copy(f.at[0, :, 8:24, first + k, :], rows.at[p, k], sem.at[p, k])
                )
        for c in copies:
            c.start()
        return copies

    def row_of(p):
        return lambda k, c: pltpu.roll(rows[p, k, c], 12, 0)

    @pl.when(jnp.logical_not(goes_up))
    def _():
        copies = load(0)
        for p in range(2):
            copies[2 * p].wait()
            copies[2 * p + 1].wait()
            row = row_of(p)
            ex, ey, ez = row(0, 0), row(0, 1), row(0, 2)
            ex_n, ez_n = row(1, 0), row(1, 2)
            hx = row(0, 3) - COURANT * ((ez_n - ez) - (roll_up(ey) - ey))
            hy = row(0, 4) - COURANT * ((roll_up(ex) - ex) - (x_up(ez) - ez))
            hz = row(0, 5) - COURANT * ((x_up(ey) - ey) - (ex_n - ex))
            cx = hz - (hy - roll_down(hy))
            cz = (hy - x_down(hy)) - hx
            base = p * DOWN_ROWS
            out[base : base + 8] = ex[0:8]
            out[base + 8 : base + 16] = ez[0:8]
            out[base + 16 : base + 24] = cx[0:8]
            out[base + 24 : base + 32] = cz[0:8]
            extra = jnp.where((tile == 1) | (tile == 2), pltpu.roll(ex[8:16], 2, 0), ez[8:16])
            out[base + 32 : base + 40] = jnp.where(tile == 3, pltpu.roll(cz[8:16], 4, 0), extra)

    @pl.when(goes_up)
    def _():
        copies = load(6)
        for p in range(2):
            copies[2 * p].wait()
            copies[2 * p + 1].wait()
            row = row_of(p)
            ex_l, ey_l, ez_l = row(0, 0), row(0, 1), row(0, 2)
            ex, ey, ez = row(1, 0), row(1, 1), row(1, 2)
            u1 = (x_up(ey) - ey) + ex
            u2 = ez + (roll_up(ey) - ey)
            hx = row(1, 3) + COURANT * u2
            hy = row(1, 4) - COURANT * ((roll_up(ex) - ex) - (x_up(ez) - ez))
            hz = row(1, 5) - COURANT * u1
            hx_l = row(0, 3) - COURANT * ((ez - ez_l) - (roll_up(ey_l) - ey_l))
            hz_l = row(0, 5) - COURANT * ((x_up(ey_l) - ey_l) - (ex - ex_l))
            cx = (hz - hz_l) - (hy - roll_down(hy))
            cy = (hx - roll_down(hx)) - (hz - x_down(hz))
            cz = (hy - x_down(hy)) - (hx - hx_l)
            base = p * UP_ROWS
            for k, v in enumerate((hx, hz, u1, u2, cx, cy, cz)):
                out[base + 8 * k : base + 8 * k + 8] = v[0:8]
            extra = jnp.where((tile == 1) | (tile == 2), pltpu.roll(hz[8:16], 2, 0), hx[8:16])
            out[base + 56 : base + 64] = jnp.where(tile == 3, pltpu.roll(cy[8:16], 3, 0), extra)


def stage_kernel(after, ff, af, field, sem):
    copies = []
    for p, f in enumerate((ff, af)):
        copies.append(
            (
                pltpu.make_async_copy(f.at[0, :, 12:22], field.at[p, :, 0:10], sem.at[p, 0]),
                pltpu.make_async_copy(f.at[0, :, 10:12], field.at[p, :, 14:16], sem.at[p, 1]),
            )
        )
    for pair in copies:
        pair[0].start()
        pair[1].start()
    last_row = sublanes((8, NX)) == 7

    def y_up(f):
        return jnp.where(last_row, 0.0, roll_up(f))

    for p in range(2):
        copies[p][0].wait()
        copies[p][1].wait()
        for z in range(10, 21):
            k, n = slot(z), slot(z + 1)
            ex, ey, ez = field[p, 0, k], field[p, 1, k], field[p, 2, k]
            field[p, 3, k] -= COURANT * ((y_up(ez) - ez) - (field[p, 1, n] - ey))
            field[p, 4, k] -= COURANT * ((field[p, 0, n] - ex) - (x_up(ez) - ez))
            if z > 10:
                field[p, 5, k] -= COURANT * ((x_up(ey) - ey) - (y_up(ex) - ex))


def from_neighbours(ev, od, below, above, below_rows, above_rows, sem):
    even = lax.axis_index("space") % 2 == 0

    def get(from_below, from_above):
        a = pltpu.make_async_copy(from_below.at[below_rows], below, sem.at[0])
        b = pltpu.make_async_copy(from_above.at[above_rows], above, sem.at[1])
        a.start()
        b.start()
        a.wait()
        b.wait()

    @pl.when(even)
    def _():
        get(od, ev)

    @pl.when(jnp.logical_not(even))
    def _():
        get(ev, od)


def cyclic_rows(shape):
    i = sublanes(shape)
    return jnp.where(i < 12, i, i - 16)


def window_start(first):
    return pl.multiple_of(jnp.clip((first // 128) * 128, 0, NX - 256), 128)


def layer_inverse(z, middle):
    if z < SLAB:
        return 1.0 / OXIDE
    if z >= SLAB + DZ:
        return 1.0
    return middle


def material_kernel(
    grid_rows, fp, ev, od, own, monitor, shape_yz, ff,
    inv_out, design_out, part_out, wide, fw, win_sem,
):
    strip, group = lax.axis_index("space"), lax.axis_index("exc")
    plane = fp[0, 37].astype(jnp.int32)
    w0 = window_start(plane - 2)
    window = pltpu.make_async_copy(ff.at[0, :, :, :, pl.ds(w0, 256)], fw, win_sem)
    window.start()
    even = strip % 2 == 0
    both = jnp.concatenate(
        [jnp.where(even, od[...], ev[...]), own[...], jnp.where(even, ev[...], od[...])], 0
    )
    kinds = both[4:20, NX:]
    for k in range(4):
        at = pl.ds(pl.multiple_of((group ^ k) * 256, 128), 256)
        wide[:, at] = both[:, 256 * k : 256 * k + 256]
    filtered = x_smooth(y_smooth(wide[...], 16))
    lower = math.tanh(SHARPNESS * MIDPOINT)
    spread = lower + math.tanh(SHARPNESS * (1.0 - MIDPOINT))
    bent = jnp.tanh(SHARPNESS * (filtered - MIDPOINT))
    projected = (lower + bent) / spread
    steepness = SHARPNESS * (1.0 - bent * bent) / spread
    mixed = OXIDE + (SILICON - OXIDE) * projected
    material = jnp.where(kinds == 2.0, mixed, jnp.where(kinds == 1.0, SILICON, OXIDE))
    inv_out[...] = pltpu.roll(1.0 / material, 12, 0)
    design = jnp.where(kinds == 2.0, steepness * fp[0, 36], 0.0)
    design_out[...] = pltpu.roll(design, 12, 0)[0:8]

    small = (16, 128)
    shift = (64 + w0 - plane + 256) % 256
    middle = pltpu.roll(inv_out[:, pl.ds(w0, 256)], shift, 1)[:, 0:128]
    rows_here = cyclic_rows(small) + ROWS * strip
    xs = lanes(small) + (plane - 64)
    inside = (rows_here >= 0) & (rows_here < grid_rows) & (xs >= 0) & (xs < NX)
    mask = jnp.where(inside, 1.0, 0.0)
    half = COURANT * mask
    ramp = 1.0 + 2.0 * (rows_here.astype(jnp.float32) + 0.5) / grid_rows
    seed_base = jnp.where(lanes(small) == 64, ramp * mask, 0.0)
    source_base = jnp.where(lanes(small) == 64, ramp, 0.0)[0:8]
    zero = jnp.zeros(small, jnp.float32)

    def at(values, z):
        return values[z] if 0 <= z < NZ else zero

    def xu(v):
        return pltpu.roll(v, 127, 1)

    def xd(v):
        return pltpu.roll(v, 1, 1)

    zs = range(NZ)
    inv = [layer_inverse(z, middle) for z in zs]
    seed = [seed_base * fp[0, z] for z in zs]
    w = [inv[z] * seed[z] for z in zs]
    hx = [half * (roll_up(w[z]) - w[z]) for z in zs]
    hy = [half * (w[z] - xu(w[z])) for z in zs]
    ex = [half * (hy[z] - at(hy, z - 1)) for z in zs]
    ey = [half * (at(hx, z - 1) - hx[z]) for z in zs]
    ez = [
        (seed[z] - COURANT * ((hy[z] - xd(hy[z])) - (hx[z] - roll_down(hx[z])))) * mask for z in zs
    ]
    wx = [inv[z] * ex[z] for z in zs]
    wy = [inv[z] * ey[z] for z in zs]
    wz = [inv[z] * ez[z] for z in zs]
    hx2 = [hx[z] + half * ((roll_up(wz[z]) - wz[z]) - (at(wy, z + 1) - wy[z])) for z in zs]
    hy2 = [hy[z] + half * ((at(wx, z + 1) - wx[z]) - (xu(wz[z]) - wz[z])) for z in zs]
    hz2 = [half * ((xu(wy[z]) - wy[z]) - (roll_up(wx[z]) - wx[z])) for z in zs]
    window.wait()
    one = jnp.zeros((8, 128), jnp.float32)
    two = jnp.zeros((8, 128), jnp.float32)
    c0, s0, c1, s1 = fp[0, 32], fp[0, 33], fp[0, 34], fp[0, 35]
    for z in zs:
        ex2 = ex[z] - half * (
            (hz2[z] - roll_down(hz2[z])) - (hy2[z] - at(hy2, z - 1))
        )
        ey2 = ey[z] - half * ((hx2[z] - at(hx2, z - 1)) - (hz2[z] - xd(hz2[z])))
        ez2 = ez[z] - half * ((hy2[z] - xd(hy2[z])) - (hx2[z] - roll_down(hx2[z])))
        f = [pltpu.roll(fw[c, z], shift, 1)[:, 0:128] for c in range(6)]
        one += ex[z][0:8] * f[0] + ey[z][0:8] * f[1] + ez[z][0:8] * f[2]
        one += hx[z][0:8] * f[3] + hy[z][0:8] * f[4]
        two += ex2[0:8] * f[0] + ey2[0:8] * f[1] + ez2[0:8] * f[2]
        two += hx2[z][0:8] * f[3] + hy2[z][0:8] * f[4] + hz2[z][0:8] * f[5]
        pulse = source_base * (COURANT * fp[0, z])
        one -= pulse * (w[z][0:8] * c0)
        two -= pulse * (wz[z][0:8] * c0 + w[z][0:8] * c1)
    total_1, total_2 = jnp.sum(one), jnp.sum(two)
    real = jnp.sum(monitor[0, 0] * shape_yz[...]) + c0 * total_1 + c1 * total_2
    imaginary = jnp.sum(monitor[0, 1] * shape_yz[...]) - s0 * total_1 - s1 * total_2
    ids = lanes((8, 128))
    part_out[...] = jnp.where(ids == 0, real, jnp.where(ids == 1, imaginary, 0.0))


def main_kernel(
    strips, grid_rows, fp, ev, od, staged, fs, asums, inv_ref, design,
    ev_out, od_out, s_out, p_out,
    field, sums, below, above, hmx, hmz, hmx2, hmz2, ezp, exp, pscr, sem, halo_sem,
):
    strip = lax.axis_index("space")
    source, plane = fp[0, 37].astype(jnp.int32), fp[0, 38].astype(jnp.int32)
    c0, s0, c1, s1 = fp[0, 32], fp[0, 33], fp[0, 34], fp[0, 35]
    sum_copies = [
        pltpu.make_async_copy(f.at[0], sums.at[p], sem.at[p, 2]) for p, f in enumerate((fs, asums))
    ]
    for p in range(2):
        sum_copies[p].start()
    from_neighbours(
        ev, od, below, above, pl.ds(0, 2 * UP_ROWS), pl.ds(0, 2 * DOWN_ROWS), halo_sem
    )
    full = (8, NX)
    row_ids = sublanes(full)
    ids = lanes(full)
    first_row, last_row = row_ids == 0, row_ids == 7
    has_below = jnp.where(strip > 0, 1.0, 0.0)
    has_above = jnp.where(strip < strips - 1, 1.0, 0.0)
    base_row = (ROWS * strip).astype(jnp.float32)
    step = 2.0 / grid_rows
    ramp = 1.0 + step * (base_row + row_ids.astype(jnp.float32) + 0.5)
    pulse = jnp.where(ids == source, ramp, 0.0)
    sine_rows = jnp.zeros(full, jnp.float32)
    for k in range(8):
        sine_rows = jnp.where(row_ids == k, fp[0, SLAB + k], sine_rows)
    sine_rows = jnp.where(ids == source, sine_rows, 0.0)
    ramp_above = 1.0 + step * (base_row + 8.5)
    ramp_below = 1.0 + step * (base_row - 0.5)
    inv_below = inv_ref[15:16]
    inv_above = inv_ref[8:9]

    def y_up(f, halo):
        return jnp.where(last_row, halo, roll_up(f))

    def y_down(f, halo):
        return jnp.where(first_row, halo, roll_down(f))

    for p in range(2):
        up0 = p * UP_ROWS
        down0 = p * DOWN_ROWS
        forward = p == 0

        def get(c, z, p=p):
            return field[p, c, slot(z)]

        def strip_row(c, r, p=p):
            return field[p, c, :, r, :]

        def start(c, z, p=p):
            return staged[p, c, slot(z)]

        def ex0_above(z):
            k = down0 + z - SLAB if 12 <= z <= 19 else down0 + 32 + {20: 2, 11: 1}[z]
            return above[k : k + 1]

        def ez0_above(z):
            k = down0 + 8 + z - SLAB if 12 <= z <= 19 else down0 + 32 + {20: 0, 11: 7, 10: 6}[z]
            return above[k : k + 1]

        for z in range(10, 21):
            k = slot(z)
            field[p, 3, k] = start(3, z) - jnp.where(last_row, COURANT * ez0_above(z), 0.0)
            if z > 10:
                field[p, 5, k] = start(5, z) + jnp.where(last_row, COURANT * ex0_above(z), 0.0)
        dhx = -COURANT * staged[p, 2, :, 0, :]
        dhz = COURANT * staged[p, 0, :, 0, :]
        block = [below[up0 + 8 * k : up0 + 8 * k + 8] for k in range(8)]
        extra = block[7]
        hmx[0:8] = has_below * (block[0] + dhx[0:8])
        hmx[8:16] = has_below * (extra + dhx[8:16])
        hmz[0:8] = has_below * (block[1] + dhz[0:8])
        hmz[8:16] = has_below * (pltpu.roll(extra, 6, 0) + dhz[8:16])
        cx = block[4] + dhz[0:8]
        cy = jnp.concatenate([block[5], pltpu.roll(extra, 5, 0)], 0)
        cy = cy + (dhx - roll_down(dhx)) - (dhz - x_down(dhz))
        cz = block[6] - dhx[0:8]
        if forward:
            cz = cz - sine_rows * (c0 * ramp_below)
        both = jnp.concatenate([cy[0:8] * inv_below, cy[8:16]], 0)
        t1 = block[2] + COURANT * ((x_up(both[0:8]) - both[0:8]) + inv_below * cx)
        t2 = block[3] + COURANT * (inv_below * cz + (roll_up(both) - both)[0:8])
        hx7, hz7 = strip_row(3, 7), strip_row(5, 7)
        ab = [above[down0 + 8 * k : down0 + 8 * k + 8] for k in range(5)]
        exp[...] = has_above * (ab[0] + COURANT * inv_above * (ab[2] - hz7[0:8]))
        drive = ab[3] + hx7[0:8]
        if forward:
            drive = drive - sine_rows * (c0 * ramp_above)
        ezp[0:8] = has_above * (ab[1] + COURANT * inv_above * drive)
        drive = ab[4][3:4] + hx7[15:16]
        if forward:
            here = lanes((1, NX)) == source
            drive = drive - jnp.where(here, fp[0, 11] * (c0 * ramp_above), 0.0)
        ezp[15:16] = has_above * (ab[4][7:8] + (COURANT / OXIDE) * drive)
        for z in range(11, 21):
            k = slot(z)
            scale = COURANT * layer_inverse(z, inv_ref[0:8])
            hx, hy, hz = get(3, z), start(4, z), get(5, z)
            ex = start(0, z) + scale * ((hz - y_down(hz, hmz[k : k + 1])) - (hy - start(4, z - 1)))
            ey = start(1, z) + scale * ((hx - get(3, z - 1)) - (hz - x_down(hz)))
            field[p, 0, k] = ex
            field[p, 1, k] = ey
            if z < 20:
                curl = (hy - x_down(hy)) - (hx - y_down(hx, hmx[k : k + 1]))
                if forward:
                    curl = curl - pulse * (fp[0, z] * c0)
                field[p, 2, k] = start(2, z) + scale * curl
        hmx2[...] = has_below * (hmx[0:8] - COURANT * (strip_row(2, 0)[0:8] - t2))
        hmz2[...] = has_below * (hmz[0:8] - COURANT * (t1 - strip_row(0, 0)[0:8]))
        for z in range(11, 20):
            k = slot(z)
            ex, ey, ez = get(0, z), get(1, z), get(2, z)
            field[p, 3, k] = get(3, z) - COURANT * (
                (y_up(ez, ezp[k : k + 1]) - ez) - (get(1, z + 1) - ey)
            )
            field[p, 4, k] = start(4, z) - COURANT * ((get(0, z + 1) - ex) - (x_up(ez) - ez))
            if z > 11:
                field[p, 5, k] = get(5, z) - COURANT * (
                    (x_up(ey) - ey) - (y_up(ex, exp[k : k + 1]) - ex)
                )
        sum_copies[p].wait()
        scale = COURANT * inv_ref[0:8]
        total = jnp.zeros(full, jnp.float32)
        for z in range(12, 20):
            k = slot(z)
            hx, hy, hz = get(3, z), get(4, z), get(5, z)
            curl_z = (hy - x_down(hy)) - (hx - y_down(hx, hmx2[k : k + 1]))
            if forward:
                curl_z = curl_z - pulse * (fp[0, z] * c1)
            curls = (
                (hz - y_down(hz, hmz2[k : k + 1])) - (hy - get(4, z - 1)),
                (hx - get(3, z - 1)) - (hz - x_down(hz)),
                curl_z,
            )
            for c in range(3):
                early = get(c, z)
                late = early + scale * curls[c]
                real = sums[p, c, k] + c0 * early + c1 * late
                imaginary = sums[p, 3 + c, k] - s0 * early - s1 * late
                if forward:
                    sums[0, c, k] = real
                    sums[0, 3 + c, k] = imaginary
                else:
                    total = total + (sums[0, c, k] * real - sums[0, 3 + c, k] * imaginary)

    w1 = window_start(plane - 1)
    wide = (16, 256)
    rows_here = cyclic_rows(wide) + ROWS * strip
    valid = (rows_here >= 0) & (rows_here < grid_rows)
    keep = jnp.where(valid, 1.0, 0.0)
    ramps = 1.0 + step * (rows_here.astype(jnp.float32) + 0.5)
    spot = jnp.where(valid & (lanes(wide) + w1 == plane), ramps, 0.0)
    inv_w = inv_ref[:, pl.ds(w1, 256)]
    own_scale = COURANT * inv_w[0:8]
    drive_0 = jnp.zeros((8, 256), jnp.float32)
    drive_1 = jnp.zeros((8, 256), jnp.float32)
    hx_last = hy_last = None
    for z in range(11, 20):
        d1 = spot * layer_inverse(z, inv_w) * (-COURANT * fp[0, z])
        hy = COURANT * (x_up(d1[0:8]) - d1[0:8])
        hx = keep * (-COURANT * (roll_up(d1) - d1))
        if z > 11:
            k = slot(z)
            e1z = d1[0:8]
            e2x = own_scale * (hy_last - hy)
            e2y = own_scale * (hx - hx_last)[0:8]
            e2z = e1z + own_scale * ((hy - x_down(hy)) - (hx - roll_down(hx))[0:8])
            part = [sums[0, c, k, :, pl.ds(w1, 256)] for c in range(6)]
            drive_0 += (c1 * part[0] + s1 * part[3]) * e2x
            drive_0 += (c1 * part[1] + s1 * part[4]) * e2y
            late = c1 * part[2] + s1 * part[5]
            drive_0 += (c0 * part[2] + s0 * part[5]) * e1z + late * e2z
            drive_1 += late * e1z
        hx_last, hy_last = hx, hy
    design_w = design[:, pl.ds(w1, 256)]
    s_own = total * design[...]
    pscr[:, 0:256] = drive_0 * design_w
    pscr[:, 256:512] = drive_1 * design_w
    pscr[:, 512:1024] = jnp.zeros((8, 512), jnp.float32)
    p_own = pscr[...]
    s_out[...] = s_own
    p_out[...] = p_own
    top = row_ids < 4
    to_up = jnp.where(top, pltpu.roll(s_own, 4, 0), p_own)
    to_down = jnp.where(top, s_own, pltpu.roll(p_own, 4, 0))
    even = strip % 2 == 0
    ev_out[...] = jnp.where(even, to_up, to_down)
    od_out[...] = jnp.where(even, to_down, to_up)


def final_kernel(norm, fp, ev, od, s_own, p_own, totals, keep, send, merit, scr):
    strip, group = lax.axis_index("space"), lax.axis_index("exc")
    plane = fp[0, 38].astype(jnp.int32)
    even = strip % 2 == 0
    low = jnp.where(even, od[...], ev[...])
    high = jnp.where(even, ev[...], od[...])
    sums = totals[...] + ev[4:5, 512:640]
    ids = lanes((1, 128))
    real = jnp.sum(jnp.where(ids == 0, sums, 0.0), axis=1, keepdims=True) / norm
    imaginary = jnp.sum(jnp.where(ids == 1, sums, 0.0), axis=1, keepdims=True) / norm
    both = jnp.concatenate([low[0:4], s_own[...], high[0:4]], 0)
    extra = jnp.concatenate([low[4:8, 0:512], p_own[:, 0:512], high[4:8, 0:512]], 0)
    merit[...] = jnp.broadcast_to(real * real + imaginary * imaginary, (1, 128))
    g0 = real * fp[0, 32] + imaginary * fp[0, 33]
    g1 = real * fp[0, 34] + imaginary * fp[0, 35]
    more = y_smooth(extra, 8)
    w1 = window_start(plane - 1)
    scr[...] = y_smooth(both, 8)
    scr[:, pl.ds(w1, 256)] += g0 * more[:, 0:256] + g1 * more[:, 256:512]
    result = x_smooth(scr[...])
    count = keep.shape[0]
    width = NX // (2 * count)

    def split(mine):
        for k in range(count):
            a = (2 * k + mine) * width
            b = (2 * k + 1 - mine) * width
            keep[k] = result[:, a : a + width]
            send[k] = result[:, b : b + width]

    @pl.when(group % 2 == 0)
    def _():
        split(0)

    @pl.when(group % 2 == 1)
    def _():
        split(1)


def params(limit=VMEM_LIMIT):
    return pltpu.CompilerParams(vmem_limit_bytes=limit)


def swap(value, axis, pairs):
    return lax.ppermute(value, axis, pairs)


def local(
    forward_fields, forward_sums, adjoint_fields, adjoint_sums, monitor_sums, density, labels,
    source_plane, monitor_plane, mode_numbers, frequency, start_phase,
):
    groups = lax.axis_size("exc")
    strips = lax.axis_size("space")
    grid_rows = ROWS * strips
    group = lax.axis_index("exc").astype(jnp.int32)
    f32 = jnp.float32

    def shaped(*shape):
        return jax.ShapeDtypeStruct(shape, f32)

    even_pairs = [(i, i ^ 1) for i in range(strips)]
    odd_pairs = [(i, ((i - 1) ^ 1) + 1) for i in range(1, strips - 1)]

    fp, shape_yz = pl.pallas_call(
        lambda *refs: prepare_kernel(grid_rows, (SILICON - OXIDE) / math.sqrt(groups * DZ), *refs),
        out_shape=[shaped(1, 128), shaped(ROWS, NZ)],
        in_specs=[VMEM_SPEC] * 5,
        out_specs=[VMEM_SPEC] * 2,
        name="prepare",
    )(
        *(
            value.reshape(1, 1)
            for value in (mode_numbers, frequency, start_phase, source_plane, monitor_plane)
        )
    )

    quarter = density.T
    width = quarter.shape[1]
    second = swap(quarter, "exc", [(i, i ^ 1) for i in range(groups)])
    across = swap(quarter, "exc", [(i, i ^ 2) for i in range(groups)])
    third = swap(second, "exc", [(i, i ^ 2) for i in range(groups)])
    small = jnp.concatenate([quarter, second, across, third, labels.astype(f32)], 1)
    od_small = swap(small, "space", odd_pairs)
    ev_small = swap(small, "space", even_pairs)

    def pack(even_goes_up, after, name):
        return pl.pallas_call(
            lambda *refs: pack_kernel(even_goes_up, *refs),
            out_shape=shaped(PACK, NX),
            in_specs=[ANY_SPEC] * 3,
            out_specs=VMEM_SPEC,
            scratch_shapes=[
                pltpu.VMEM((2, 2, 6, 16, NX), f32),
                pltpu.SemaphoreType.DMA((2, 2)),
            ],
            compiler_params=params(PACK_LIMIT),
            name=name,
        )(after, forward_fields, adjoint_fields)

    od = pack(False, second, "pack_odd")
    ev = pack(True, third, "pack_even")
    staged = pl.pallas_call(
        stage_kernel,
        out_shape=shaped(2, 6, 16, ROWS, NX),
        in_specs=[ANY_SPEC] * 3,
        out_specs=VMEM_SPEC,
        scratch_shapes=[pltpu.SemaphoreType.DMA((2, 2))],
        compiler_params=params(46 * 1024 * 1024),
        name="stage",
    )(small, forward_fields, adjoint_fields)
    od = swap(od, "space", odd_pairs)
    ev = swap(ev, "space", even_pairs)

    fp, staged = lax.optimization_barrier((fp, staged))

    def material(*refs):
        material_kernel(grid_rows, *refs)

    inv, design, part = pl.pallas_call(
        material,
        out_shape=[shaped(16, NX), shaped(8, NX), shaped(8, 128)],
        in_specs=[SMEM_SPEC] + [VMEM_SPEC] * 5 + [ANY_SPEC],
        out_specs=[VMEM_SPEC] * 3,
        scratch_shapes=[
            pltpu.VMEM((24, NX), f32),
            pltpu.VMEM((6, NZ, ROWS, 256), f32),
            pltpu.SemaphoreType.DMA,
        ],
        compiler_params=params(),
        name="material",
    )(
        fp, ev_small, od_small, small, monitor_sums.transpose(0, 1, 3, 2), shape_yz,
        forward_fields,
    )

    totals = part[0:1]

    def fold(totals, bit):
        return totals + swap(totals, "space", [(i, i ^ bit) for i in range(strips)])

    arriving = swap(totals, "space", [(i, i ^ 4) for i in range(strips)])
    def main(*refs):
        main_kernel(strips, grid_rows, *refs)

    ev3, od3, s_own, p_own = pl.pallas_call(
        main,
        out_shape=[shaped(8, NX)] * 4,
        in_specs=[SMEM_SPEC] + [ANY_SPEC] * 2 + [VMEM_SPEC] + [ANY_SPEC] * 2 + [VMEM_SPEC] * 2,
        out_specs=[VMEM_SPEC] * 4,
        scratch_shapes=[
            pltpu.VMEM((2, 6, 16, ROWS, NX), f32),
            pltpu.VMEM((2, 6, DZ, ROWS, NX), f32),
            pltpu.VMEM((2 * UP_ROWS, NX), f32),
            pltpu.VMEM((2 * DOWN_ROWS, NX), f32),
            pltpu.VMEM((16, NX), f32),
            pltpu.VMEM((16, NX), f32),
            pltpu.VMEM((8, NX), f32),
            pltpu.VMEM((8, NX), f32),
            pltpu.VMEM((16, NX), f32),
            pltpu.VMEM((8, NX), f32),
            pltpu.VMEM((8, NX), f32),
            pltpu.SemaphoreType.DMA((2, 3)),
            pltpu.SemaphoreType.DMA((2,)),
        ],
        compiler_params=params(),
        name="main",
    )(
        fp, ev, od, staged, forward_sums, adjoint_sums, inv, design,
    )
    od3, totals = lax.optimization_barrier((od3, totals))
    totals = totals + arriving
    od3 = swap(od3, "space", odd_pairs)
    totals = fold(totals, 8)
    totals = fold(totals, 24)
    totals = fold(totals, 3)
    ev3 = swap(lax.dynamic_update_slice(ev3, totals, (4, 512)), "space", even_pairs)

    norm = math.sqrt(NZ * grid_rows)
    half_count = groups // 2

    def final(*refs):
        final_kernel(norm, *refs)

    keep, send, merit = pl.pallas_call(
        final,
        out_shape=[shaped(half_count, ROWS, width)] * 2 + [shaped(1, 128)],
        in_specs=[SMEM_SPEC] + [VMEM_SPEC] * 5,
        out_specs=[VMEM_SPEC] * 3,
        scratch_shapes=[pltpu.VMEM((8, NX), f32)],
        compiler_params=params(),
        name="final",
    )(fp, ev3, od3, s_own, p_own, totals)
    block = keep + swap(send, "exc", [(i, i ^ 1) for i in range(groups)])
    bit = 2
    while bit < groups:
        count = block.shape[0] // 2
        pairs = block.reshape(count, 2, ROWS, width)
        mine = (group // bit) % 2
        kept = lax.dynamic_index_in_dim(pairs, mine, 1, keepdims=False)
        given = lax.dynamic_index_in_dim(pairs, 1 - mine, 1, keepdims=False)
        block = kept + swap(given, "exc", [(i, i ^ bit) for i in range(groups)])
        bit *= 2
    return block[0].T, merit[0, 0:1]


def solution(mesh):
    in_specs = (
        P("exc", None, None, "space", None),
        P("exc", None, None, "space", None),
        P("exc", None, None, "space", None),
        P("exc", None, None, "space", None),
        P("exc", None, None, "space"),
        P("exc", "space"),
        P("space", None),
        P("exc"),
        P("exc"),
        P("exc"),
        P("exc"),
        P("exc"),
    )
    out_specs = (P("exc", "space"), P("exc"))
    return jax.shard_map(local, mesh=mesh, in_specs=in_specs, out_specs=out_specs, check_vma=False)
```

```python
import math

import jax
import jax.numpy as jnp
from jax import lax
from jax.experimental import pallas as pl
from jax.experimental.pallas import tpu as pltpu
from jax.sharding import PartitionSpec as P

R = 4
COURANT = 0.5
OXIDE = 2.1
SILICON = 12.1
SHARPNESS = 4.0
MIDPOINT = 0.5

ROWS = 8
NX = 1024
NZ = 32
SLAB = 12
DZ = 8
UP_ROWS = 64
DOWN_ROWS = 40
PACK = 2 * UP_ROWS
WEIGHTS = [(R + 1.0 - abs(k - R)) / ((R + 1.0) * (R + 1.0)) for k in range(2 * R + 1)]
VMEM_LIMIT = 32 * 1024 * 1024
PACK_LIMIT = 50 * 1024 * 1024

SMEM_SPEC = pl.BlockSpec(memory_space=pltpu.SMEM)
VMEM_SPEC = pl.BlockSpec(memory_space=pltpu.VMEM)
ANY_SPEC = pl.BlockSpec(memory_space=pl.ANY)


def slot(z):
    return (z - SLAB) % 16


def lanes(shape):
    return lax.broadcasted_iota(jnp.int32, shape, len(shape) - 1)


def sublanes(shape):
    return lax.broadcasted_iota(jnp.int32, shape, len(shape) - 2)


def x_up(f):
    n = f.shape[-1]
    return jnp.where(lanes(f.shape) == n - 1, 0.0, pltpu.roll(f, n - 1, len(f.shape) - 1))


def x_down(f):
    return jnp.where(lanes(f.shape) == 0, 0.0, pltpu.roll(f, 1, len(f.shape) - 1))


def roll_up(f):
    return pltpu.roll(f, f.shape[0] - 1, 0)


def roll_down(f):
    return pltpu.roll(f, 1, 0)


def y_smooth(f, count):
    total = None
    for k, w in enumerate(WEIGHTS):
        part = w * f[k : k + count]
        total = part if total is None else total + part
    return total


def x_smooth(f):
    n = f.shape[-1]
    ids = lanes(f.shape)
    total = WEIGHTS[R] * f
    for a in range(1, R + 1):
        ahead = jnp.where(ids < n - a, pltpu.roll(f, n - a, 1), 0.0)
        behind = jnp.where(ids >= a, pltpu.roll(f, a, 1), 0.0)
        total = total + WEIGHTS[R + a] * (ahead + behind)
    return total


def prepare_kernel(grid_rows, scale, mode_at, rate_at, phase_at, source_at, monitor_at, fp, shape_yz):
    order = math.pi * (mode_at[...] + 1).astype(jnp.float32)
    rate, phase = rate_at[...], phase_at[...]
    number = lanes((1, 128))
    early, late = phase, phase + rate
    angle = jnp.where(number < 34, early, late)
    angle = jnp.where(number < NZ, order * (number.astype(jnp.float32) + 0.5) / NZ, angle)
    value = jnp.where((number == 32) | (number == 34), jnp.cos(angle), jnp.sin(angle))
    value = jnp.where(number == 36, rate * rate * scale, value)
    value = jnp.where(number == 37, source_at[...].astype(jnp.float32), value)
    fp[...] = jnp.where(number == 38, monitor_at[...].astype(jnp.float32), value)
    small = (ROWS, NZ)
    rows = lax.axis_index("space") * ROWS + sublanes(small)
    ramp = 1.0 + 2.0 * (rows.astype(jnp.float32) + 0.5) / grid_rows
    shape_yz[...] = ramp * jnp.sin(order * (lanes(small).astype(jnp.float32) + 0.5) / NZ)


def pack_kernel(even_goes_up, after, ff, af, out, rows, sem):
    tile = sublanes((8, NX))
    even = lax.axis_index("space") % 2 == 0
    goes_up = even if even_goes_up else jnp.logical_not(even)

    def load(first):
        copies = []
        for p, f in enumerate((ff, af)):
            for k in range(2):
                copies.append(
                    pltpu.make_async_copy(f.at[0, :, 8:24, first + k, :], rows.at[p, k], sem.at[p, k])
                )
        for c in copies:
            c.start()
        return copies

    def row_of(p):
        return lambda k, c: pltpu.roll(rows[p, k, c], 12, 0)

    @pl.when(jnp.logical_not(goes_up))
    def _():
        copies = load(0)
        for p in range(2):
            copies[2 * p].wait()
            copies[2 * p + 1].wait()
            row = row_of(p)
            ex, ey, ez = row(0, 0), row(0, 1), row(0, 2)
            ex_n, ez_n = row(1, 0), row(1, 2)
            hx = row(0, 3) - COURANT * ((ez_n - ez) - (roll_up(ey) - ey))
            hy = row(0, 4) - COURANT * ((roll_up(ex) - ex) - (x_up(ez) - ez))
            hz = row(0, 5) - COURANT * ((x_up(ey) - ey) - (ex_n - ex))
            cx = hz - (hy - roll_down(hy))
            cz = (hy - x_down(hy)) - hx
            base = p * DOWN_ROWS
            out[base : base + 8] = ex[0:8]
            out[base + 8 : base + 16] = ez[0:8]
            out[base + 16 : base + 24] = cx[0:8]
            out[base + 24 : base + 32] = cz[0:8]
            extra = jnp.where((tile == 1) | (tile == 2), pltpu.roll(ex[8:16], 2, 0), ez[8:16])
            out[base + 32 : base + 40] = jnp.where(tile == 3, pltpu.roll(cz[8:16], 4, 0), extra)

    @pl.when(goes_up)
    def _():
        copies = load(6)
        for p in range(2):
            copies[2 * p].wait()
            copies[2 * p + 1].wait()
            row = row_of(p)
            ex_l, ey_l, ez_l = row(0, 0), row(0, 1), row(0, 2)
            ex, ey, ez = row(1, 0), row(1, 1), row(1, 2)
            u1 = (x_up(ey) - ey) + ex
            u2 = ez + (roll_up(ey) - ey)
            hx = row(1, 3) + COURANT * u2
            hy = row(1, 4) - COURANT * ((roll_up(ex) - ex) - (x_up(ez) - ez))
            hz = row(1, 5) - COURANT * u1
            hx_l = row(0, 3) - COURANT * ((ez - ez_l) - (roll_up(ey_l) - ey_l))
            hz_l = row(0, 5) - COURANT * ((x_up(ey_l) - ey_l) - (ex - ex_l))
            cx = (hz - hz_l) - (hy - roll_down(hy))
            cy = (hx - roll_down(hx)) - (hz - x_down(hz))
            cz = (hy - x_down(hy)) - (hx - hx_l)
            base = p * UP_ROWS
            for k, v in enumerate((hx, hz, u1, u2, cx, cy, cz)):
                out[base + 8 * k : base + 8 * k + 8] = v[0:8]
            extra = jnp.where((tile == 1) | (tile == 2), pltpu.roll(hz[8:16], 2, 0), hx[8:16])
            out[base + 56 : base + 64] = jnp.where(tile == 3, pltpu.roll(cy[8:16], 3, 0), extra)


def stage_kernel(after, ff, af, field, sem):
    copies = []
    for p, f in enumerate((ff, af)):
        copies.append(
            (
                pltpu.make_async_copy(f.at[0, :, 12:22], field.at[p, :, 0:10], sem.at[p, 0]),
                pltpu.make_async_copy(f.at[0, :, 10:12], field.at[p, :, 14:16], sem.at[p, 1]),
            )
        )
    for pair in copies:
        pair[0].start()
        pair[1].start()
    last_row = sublanes((8, NX)) == 7

    def y_up(f):
        return jnp.where(last_row, 0.0, roll_up(f))

    for p in range(2):
        copies[p][0].wait()
        copies[p][1].wait()
        for z in range(10, 21):
            k, n = slot(z), slot(z + 1)
            ex, ey, ez = field[p, 0, k], field[p, 1, k], field[p, 2, k]
            field[p, 3, k] -= COURANT * ((y_up(ez) - ez) - (field[p, 1, n] - ey))
            field[p, 4, k] -= COURANT * ((field[p, 0, n] - ex) - (x_up(ez) - ez))
            if z > 10:
                field[p, 5, k] -= COURANT * ((x_up(ey) - ey) - (y_up(ex) - ex))


def from_neighbours(ev, od, below, above, below_rows, above_rows, sem):
    even = lax.axis_index("space") % 2 == 0

    def get(from_below, from_above):
        a = pltpu.make_async_copy(from_below.at[below_rows], below, sem.at[0])
        b = pltpu.make_async_copy(from_above.at[above_rows], above, sem.at[1])
        a.start()
        b.start()
        a.wait()
        b.wait()

    @pl.when(even)
    def _():
        get(od, ev)

    @pl.when(jnp.logical_not(even))
    def _():
        get(ev, od)


def cyclic_rows(shape):
    i = sublanes(shape)
    return jnp.where(i < 12, i, i - 16)


def window_start(first):
    return pl.multiple_of(jnp.clip((first // 128) * 128, 0, NX - 256), 128)


def layer_inverse(z, middle):
    if z < SLAB:
        return 1.0 / OXIDE
    if z >= SLAB + DZ:
        return 1.0
    return middle


def material_kernel(
    grid_rows, fp, ev, od, own, monitor, shape_yz, ff,
    inv_out, design_out, part_out, wide, fw, win_sem,
):
    strip, group = lax.axis_index("space"), lax.axis_index("exc")
    plane = fp[0, 37].astype(jnp.int32)
    w0 = window_start(plane - 2)
    window = pltpu.make_async_copy(ff.at[0, :, :, :, pl.ds(w0, 256)], fw, win_sem)
    window.start()
    even = strip % 2 == 0
    both = jnp.concatenate(
        [jnp.where(even, od[...], ev[...]), own[...], jnp.where(even, ev[...], od[...])], 0
    )
    kinds = both[4:20, NX:]
    for k in range(4):
        at = pl.ds(pl.multiple_of((group ^ k) * 256, 128), 256)
        wide[:, at] = both[:, 256 * k : 256 * k + 256]
    filtered = x_smooth(y_smooth(wide[...], 16))
    lower = math.tanh(SHARPNESS * MIDPOINT)
    spread = lower + math.tanh(SHARPNESS * (1.0 - MIDPOINT))
    bent = jnp.tanh(SHARPNESS * (filtered - MIDPOINT))
    projected = (lower + bent) / spread
    steepness = SHARPNESS * (1.0 - bent * bent) / spread
    mixed = OXIDE + (SILICON - OXIDE) * projected
    material = jnp.where(kinds == 2.0, mixed, jnp.where(kinds == 1.0, SILICON, OXIDE))
    inv_out[...] = pltpu.roll(1.0 / material, 12, 0)
    design = jnp.where(kinds == 2.0, steepness * fp[0, 36], 0.0)
    design_out[...] = pltpu.roll(design, 12, 0)[0:8]

    small = (16, 128)
    shift = (64 + w0 - plane + 256) % 256
    middle = pltpu.roll(inv_out[:, pl.ds(w0, 256)], shift, 1)[:, 0:128]
    rows_here = cyclic_rows(small) + ROWS * strip
    xs = lanes(small) + (plane - 64)
    inside = (rows_here >= 0) & (rows_here < grid_rows) & (xs >= 0) & (xs < NX)
    mask = jnp.where(inside, 1.0, 0.0)
    half = COURANT * mask
    ramp = 1.0 + 2.0 * (rows_here.astype(jnp.float32) + 0.5) / grid_rows
    seed_base = jnp.where(lanes(small) == 64, ramp * mask, 0.0)
    source_base = jnp.where(lanes(small) == 64, ramp, 0.0)[0:8]
    zero = jnp.zeros(small, jnp.float32)

    def at(values, z):
        return values[z] if 0 <= z < NZ else zero

    def xu(v):
        return pltpu.roll(v, 127, 1)

    def xd(v):
        return pltpu.roll(v, 1, 1)

    zs = range(NZ)
    inv = [layer_inverse(z, middle) for z in zs]
    seed = [seed_base * fp[0, z] for z in zs]
    w = [inv[z] * seed[z] for z in zs]
    hx = [half * (roll_up(w[z]) - w[z]) for z in zs]
    hy = [half * (w[z] - xu(w[z])) for z in zs]
    ex = [half * (hy[z] - at(hy, z - 1)) for z in zs]
    ey = [half * (at(hx, z - 1) - hx[z]) for z in zs]
    ez = [
        (seed[z] - COURANT * ((hy[z] - xd(hy[z])) - (hx[z] - roll_down(hx[z])))) * mask for z in zs
    ]
    wx = [inv[z] * ex[z] for z in zs]
    wy = [inv[z] * ey[z] for z in zs]
    wz = [inv[z] * ez[z] for z in zs]
    hx2 = [hx[z] + half * ((roll_up(wz[z]) - wz[z]) - (at(wy, z + 1) - wy[z])) for z in zs]
    hy2 = [hy[z] + half * ((at(wx, z + 1) - wx[z]) - (xu(wz[z]) - wz[z])) for z in zs]
    hz2 = [half * ((xu(wy[z]) - wy[z]) - (roll_up(wx[z]) - wx[z])) for z in zs]
    window.wait()
    one = jnp.zeros((8, 128), jnp.float32)
    two = jnp.zeros((8, 128), jnp.float32)
    c0, s0, c1, s1 = fp[0, 32], fp[0, 33], fp[0, 34], fp[0, 35]
    for z in zs:
        ex2 = ex[z] - half * (
            (hz2[z] - roll_down(hz2[z])) - (hy2[z] - at(hy2, z - 1))
        )
        ey2 = ey[z] - half * ((hx2[z] - at(hx2, z - 1)) - (hz2[z] - xd(hz2[z])))
        ez2 = ez[z] - half * ((hy2[z] - xd(hy2[z])) - (hx2[z] - roll_down(hx2[z])))
        f = [pltpu.roll(fw[c, z], shift, 1)[:, 0:128] for c in range(6)]
        one += ex[z][0:8] * f[0] + ey[z][0:8] * f[1] + ez[z][0:8] * f[2]
        one += hx[z][0:8] * f[3] + hy[z][0:8] * f[4]
        two += ex2[0:8] * f[0] + ey2[0:8] * f[1] + ez2[0:8] * f[2]
        two += hx2[z][0:8] * f[3] + hy2[z][0:8] * f[4] + hz2[z][0:8] * f[5]
        pulse = source_base * (COURANT * fp[0, z])
        one -= pulse * (w[z][0:8] * c0)
        two -= pulse * (wz[z][0:8] * c0 + w[z][0:8] * c1)
    total_1, total_2 = jnp.sum(one), jnp.sum(two)
    real = jnp.sum(monitor[0, 0] * shape_yz[...]) + c0 * total_1 + c1 * total_2
    imaginary = jnp.sum(monitor[0, 1] * shape_yz[...]) - s0 * total_1 - s1 * total_2
    ids = lanes((8, 128))
    part_out[...] = jnp.where(ids == 0, real, jnp.where(ids == 1, imaginary, 0.0))


def main_kernel(
    strips, grid_rows, fp, ev, od, staged, fs, asums, inv_ref, design,
    ev_out, od_out, s_out, p_out,
    field, sums, below, above, hmx, hmz, hmx2, hmz2, ezp, exp, pscr, sem, halo_sem,
):
    strip = lax.axis_index("space")
    source, plane = fp[0, 37].astype(jnp.int32), fp[0, 38].astype(jnp.int32)
    c0, s0, c1, s1 = fp[0, 32], fp[0, 33], fp[0, 34], fp[0, 35]
    sum_copies = [
        pltpu.make_async_copy(f.at[0], sums.at[p], sem.at[p, 2]) for p, f in enumerate((fs, asums))
    ]
    for p in range(2):
        sum_copies[p].start()
    from_neighbours(
        ev, od, below, above, pl.ds(0, 2 * UP_ROWS), pl.ds(0, 2 * DOWN_ROWS), halo_sem
    )
    full = (8, NX)
    row_ids = sublanes(full)
    ids = lanes(full)
    first_row, last_row = row_ids == 0, row_ids == 7
    has_below = jnp.where(strip > 0, 1.0, 0.0)
    has_above = jnp.where(strip < strips - 1, 1.0, 0.0)
    base_row = (ROWS * strip).astype(jnp.float32)
    step = 2.0 / grid_rows
    ramp = 1.0 + step * (base_row + row_ids.astype(jnp.float32) + 0.5)
    pulse = jnp.where(ids == source, ramp, 0.0)
    sine_rows = jnp.zeros(full, jnp.float32)
    for k in range(8):
        sine_rows = jnp.where(row_ids == k, fp[0, SLAB + k], sine_rows)
    sine_rows = jnp.where(ids == source, sine_rows, 0.0)
    ramp_above = 1.0 + step * (base_row + 8.5)
    ramp_below = 1.0 + step * (base_row - 0.5)
    inv_below = inv_ref[15:16]
    inv_above = inv_ref[8:9]

    def y_up(f, halo):
        return jnp.where(last_row, halo, roll_up(f))

    def y_down(f, halo):
        return jnp.where(first_row, halo, roll_down(f))

    for p in range(2):
        up0 = p * UP_ROWS
        down0 = p * DOWN_ROWS
        forward = p == 0

        def get(c, z, p=p):
            return field[p, c, slot(z)]

        def strip_row(c, r, p=p):
            return field[p, c, :, r, :]

        def start(c, z, p=p):
            return staged[p, c, slot(z)]

        def ex0_above(z):
            k = down0 + z - SLAB if 12 <= z <= 19 else down0 + 32 + {20: 2, 11: 1}[z]
            return above[k : k + 1]

        def ez0_above(z):
            k = down0 + 8 + z - SLAB if 12 <= z <= 19 else down0 + 32 + {20: 0, 11: 7, 10: 6}[z]
            return above[k : k + 1]

        for z in range(10, 21):
            k = slot(z)
            field[p, 3, k] = start(3, z) - jnp.where(last_row, COURANT * ez0_above(z), 0.0)
            if z > 10:
                field[p, 5, k] = start(5, z) + jnp.where(last_row, COURANT * ex0_above(z), 0.0)
        dhx = -COURANT * staged[p, 2, :, 0, :]
        dhz = COURANT * staged[p, 0, :, 0, :]
        block = [below[up0 + 8 * k : up0 + 8 * k + 8] for k in range(8)]
        extra = block[7]
        hmx[0:8] = has_below * (block[0] + dhx[0:8])
        hmx[8:16] = has_below * (extra + dhx[8:16])
        hmz[0:8] = has_below * (block[1] + dhz[0:8])
        hmz[8:16] = has_below * (pltpu.roll(extra, 6, 0) + dhz[8:16])
        cx = block[4] + dhz[0:8]
        cy = jnp.concatenate([block[5], pltpu.roll(extra, 5, 0)], 0)
        cy = cy + (dhx - roll_down(dhx)) - (dhz - x_down(dhz))
        cz = block[6] - dhx[0:8]
        if forward:
            cz = cz - sine_rows * (c0 * ramp_below)
        both = jnp.concatenate([cy[0:8] * inv_below, cy[8:16]], 0)
        t1 = block[2] + COURANT * ((x_up(both[0:8]) - both[0:8]) + inv_below * cx)
        t2 = block[3] + COURANT * (inv_below * cz + (roll_up(both) - both)[0:8])
        hx7, hz7 = strip_row(3, 7), strip_row(5, 7)
        ab = [above[down0 + 8 * k : down0 + 8 * k + 8] for k in range(5)]
        exp[...] = has_above * (ab[0] + COURANT * inv_above * (ab[2] - hz7[0:8]))
        drive = ab[3] + hx7[0:8]
        if forward:
            drive = drive - sine_rows * (c0 * ramp_above)
        ezp[0:8] = has_above * (ab[1] + COURANT * inv_above * drive)
        drive = ab[4][3:4] + hx7[15:16]
        if forward:
            here = lanes((1, NX)) == source
            drive = drive - jnp.where(here, fp[0, 11] * (c0 * ramp_above), 0.0)
        ezp[15:16] = has_above * (ab[4][7:8] + (COURANT / OXIDE) * drive)
        for z in range(11, 21):
            k = slot(z)
            scale = COURANT * layer_inverse(z, inv_ref[0:8])
            hx, hy, hz = get(3, z), start(4, z), get(5, z)
            ex = start(0, z) + scale * ((hz - y_down(hz, hmz[k : k + 1])) - (hy - start(4, z - 1)))
            ey = start(1, z) + scale * ((hx - get(3, z - 1)) - (hz - x_down(hz)))
            field[p, 0, k] = ex
            field[p, 1, k] = ey
            if z < 20:
                curl = (hy - x_down(hy)) - (hx - y_down(hx, hmx[k : k + 1]))
                if forward:
                    curl = curl - pulse * (fp[0, z] * c0)
                field[p, 2, k] = start(2, z) + scale * curl
        hmx2[...] = has_below * (hmx[0:8] - COURANT * (strip_row(2, 0)[0:8] - t2))
        hmz2[...] = has_below * (hmz[0:8] - COURANT * (t1 - strip_row(0, 0)[0:8]))
        for z in range(11, 20):
            k = slot(z)
            ex, ey, ez = get(0, z), get(1, z), get(2, z)
            field[p, 3, k] = get(3, z) - COURANT * (
                (y_up(ez, ezp[k : k + 1]) - ez) - (get(1, z + 1) - ey)
            )
            field[p, 4, k] = start(4, z) - COURANT * ((get(0, z + 1) - ex) - (x_up(ez) - ez))
            if z > 11:
                field[p, 5, k] = get(5, z) - COURANT * (
                    (x_up(ey) - ey) - (y_up(ex, exp[k : k + 1]) - ex)
                )
        sum_copies[p].wait()
        scale = COURANT * inv_ref[0:8]
        total = jnp.zeros(full, jnp.float32)
        for z in range(12, 20):
            k = slot(z)
            hx, hy, hz = get(3, z), get(4, z), get(5, z)
            curl_z = (hy - x_down(hy)) - (hx - y_down(hx, hmx2[k : k + 1]))
            if forward:
                curl_z = curl_z - pulse * (fp[0, z] * c1)
            curls = (
                (hz - y_down(hz, hmz2[k : k + 1])) - (hy - get(4, z - 1)),
                (hx - get(3, z - 1)) - (hz - x_down(hz)),
                curl_z,
            )
            for c in range(3):
                early = get(c, z)
                late = early + scale * curls[c]
                real = sums[p, c, k] + c0 * early + c1 * late
                imaginary = sums[p, 3 + c, k] - s0 * early - s1 * late
                if forward:
                    sums[0, c, k] = real
                    sums[0, 3 + c, k] = imaginary
                else:
                    total = total + (sums[0, c, k] * real - sums[0, 3 + c, k] * imaginary)

    w1 = window_start(plane - 1)
    wide = (16, 256)
    rows_here = cyclic_rows(wide) + ROWS * strip
    valid = (rows_here >= 0) & (rows_here < grid_rows)
    keep = jnp.where(valid, 1.0, 0.0)
    ramps = 1.0 + step * (rows_here.astype(jnp.float32) + 0.5)
    spot = jnp.where(valid & (lanes(wide) + w1 == plane), ramps, 0.0)
    inv_w = inv_ref[:, pl.ds(w1, 256)]
    own_scale = COURANT * inv_w[0:8]
    drive_0 = jnp.zeros((8, 256), jnp.float32)
    drive_1 = jnp.zeros((8, 256), jnp.float32)
    hx_last = hy_last = None
    for z in range(11, 20):
        d1 = spot * layer_inverse(z, inv_w) * (-COURANT * fp[0, z])
        hy = COURANT * (x_up(d1[0:8]) - d1[0:8])
        hx = keep * (-COURANT * (roll_up(d1) - d1))
        if z > 11:
            k = slot(z)
            e1z = d1[0:8]
            e2x = own_scale * (hy_last - hy)
            e2y = own_scale * (hx - hx_last)[0:8]
            e2z = e1z + own_scale * ((hy - x_down(hy)) - (hx - roll_down(hx))[0:8])
            part = [sums[0, c, k, :, pl.ds(w1, 256)] for c in range(6)]
            drive_0 += (c1 * part[0] + s1 * part[3]) * e2x
            drive_0 += (c1 * part[1] + s1 * part[4]) * e2y
            late = c1 * part[2] + s1 * part[5]
            drive_0 += (c0 * part[2] + s0 * part[5]) * e1z + late * e2z
            drive_1 += late * e1z
        hx_last, hy_last = hx, hy
    design_w = design[:, pl.ds(w1, 256)]
    s_own = total * design[...]
    pscr[:, 0:256] = drive_0 * design_w
    pscr[:, 256:512] = drive_1 * design_w
    pscr[:, 512:1024] = jnp.zeros((8, 512), jnp.float32)
    p_own = pscr[...]
    s_out[...] = s_own
    p_out[...] = p_own
    top = row_ids < 4
    to_up = jnp.where(top, pltpu.roll(s_own, 4, 0), p_own)
    to_down = jnp.where(top, s_own, pltpu.roll(p_own, 4, 0))
    even = strip % 2 == 0
    ev_out[...] = jnp.where(even, to_up, to_down)
    od_out[...] = jnp.where(even, to_down, to_up)


def final_kernel(norm, fp, ev, od, s_own, p_own, totals, *outs):
    *blocks, merit, scr = outs
    strip, group = lax.axis_index("space"), lax.axis_index("exc")
    plane = fp[0, 38].astype(jnp.int32)
    even = strip % 2 == 0
    low = jnp.where(even, od[...], ev[...])
    high = jnp.where(even, ev[...], od[...])
    sums = totals[...] + ev[4:5, 512:640]
    ids = lanes((1, 128))
    real = jnp.sum(jnp.where(ids == 0, sums, 0.0), axis=1, keepdims=True) / norm
    imaginary = jnp.sum(jnp.where(ids == 1, sums, 0.0), axis=1, keepdims=True) / norm
    both = jnp.concatenate([low[0:4], s_own[...], high[0:4]], 0)
    extra = jnp.concatenate([low[4:8, 0:512], p_own[:, 0:512], high[4:8, 0:512]], 0)
    merit[...] = jnp.broadcast_to(real * real + imaginary * imaginary, (1, 128))
    g0 = real * fp[0, 32] + imaginary * fp[0, 33]
    g1 = real * fp[0, 34] + imaginary * fp[0, 35]
    more = y_smooth(extra, 8)
    w1 = window_start(plane - 1)
    scr[...] = y_smooth(both, 8)
    scr[:, pl.ds(w1, 256)] += g0 * more[:, 0:256] + g1 * more[:, 256:512]
    scr[...] = x_smooth(scr[...])
    width = NX // len(blocks)
    for k, block in enumerate(blocks):
        at = pl.multiple_of((group ^ k) * width, 128)
        block[...] = scr[:, pl.ds(at, width)]


def params(limit=VMEM_LIMIT):
    return pltpu.CompilerParams(vmem_limit_bytes=limit)


def swap(value, axis, pairs):
    return lax.ppermute(value, axis, pairs)


def local(
    forward_fields, forward_sums, adjoint_fields, adjoint_sums, monitor_sums, density, labels,
    source_plane, monitor_plane, mode_numbers, frequency, start_phase,
):
    groups = lax.axis_size("exc")
    strips = lax.axis_size("space")
    grid_rows = ROWS * strips
    f32 = jnp.float32

    def shaped(*shape):
        return jax.ShapeDtypeStruct(shape, f32)

    even_pairs = [(i, i ^ 1) for i in range(strips)]
    odd_pairs = [(i, ((i - 1) ^ 1) + 1) for i in range(1, strips - 1)]

    fp, shape_yz = pl.pallas_call(
        lambda *refs: prepare_kernel(grid_rows, (SILICON - OXIDE) / math.sqrt(groups * DZ), *refs),
        out_shape=[shaped(1, 128), shaped(ROWS, NZ)],
        in_specs=[VMEM_SPEC] * 5,
        out_specs=[VMEM_SPEC] * 2,
        name="prepare",
    )(
        *(
            value.reshape(1, 1)
            for value in (mode_numbers, frequency, start_phase, source_plane, monitor_plane)
        )
    )

    quarter = density.T
    width = quarter.shape[1]
    second = swap(quarter, "exc", [(i, i ^ 1) for i in range(groups)])
    across = swap(quarter, "exc", [(i, i ^ 2) for i in range(groups)])
    third = swap(second, "exc", [(i, i ^ 2) for i in range(groups)])
    small = jnp.concatenate([quarter, second, across, third, labels.astype(f32)], 1)
    od_small = swap(small, "space", odd_pairs)
    ev_small = swap(small, "space", even_pairs)

    def pack(even_goes_up, after, name):
        return pl.pallas_call(
            lambda *refs: pack_kernel(even_goes_up, *refs),
            out_shape=shaped(PACK, NX),
            in_specs=[ANY_SPEC] * 3,
            out_specs=VMEM_SPEC,
            scratch_shapes=[
                pltpu.VMEM((2, 2, 6, 16, NX), f32),
                pltpu.SemaphoreType.DMA((2, 2)),
            ],
            compiler_params=params(PACK_LIMIT),
            name=name,
        )(after, forward_fields, adjoint_fields)

    od = pack(False, second, "pack_odd")
    ev = pack(True, third, "pack_even")
    staged = pl.pallas_call(
        stage_kernel,
        out_shape=shaped(2, 6, 16, ROWS, NX),
        in_specs=[ANY_SPEC] * 3,
        out_specs=VMEM_SPEC,
        scratch_shapes=[pltpu.SemaphoreType.DMA((2, 2))],
        compiler_params=params(46 * 1024 * 1024),
        name="stage",
    )(small, forward_fields, adjoint_fields)
    od = swap(od, "space", odd_pairs)
    ev = swap(ev, "space", even_pairs)

    fp, staged = lax.optimization_barrier((fp, staged))

    def material(*refs):
        material_kernel(grid_rows, *refs)

    inv, design, part = pl.pallas_call(
        material,
        out_shape=[shaped(16, NX), shaped(8, NX), shaped(8, 128)],
        in_specs=[SMEM_SPEC] + [VMEM_SPEC] * 5 + [ANY_SPEC],
        out_specs=[VMEM_SPEC] * 3,
        scratch_shapes=[
            pltpu.VMEM((24, NX), f32),
            pltpu.VMEM((6, NZ, ROWS, 256), f32),
            pltpu.SemaphoreType.DMA,
        ],
        compiler_params=params(),
        name="material",
    )(
        fp, ev_small, od_small, small, monitor_sums.transpose(0, 1, 3, 2), shape_yz,
        forward_fields,
    )

    totals = part[0:1]

    def fold(totals, bit):
        return totals + swap(totals, "space", [(i, i ^ bit) for i in range(strips)])

    arriving = swap(totals, "space", [(i, i ^ 4) for i in range(strips)])
    def main(*refs):
        main_kernel(strips, grid_rows, *refs)

    ev3, od3, s_own, p_own = pl.pallas_call(
        main,
        out_shape=[shaped(8, NX)] * 4,
        in_specs=[SMEM_SPEC] + [ANY_SPEC] * 2 + [VMEM_SPEC] + [ANY_SPEC] * 2 + [VMEM_SPEC] * 2,
        out_specs=[VMEM_SPEC] * 4,
        scratch_shapes=[
            pltpu.VMEM((2, 6, 16, ROWS, NX), f32),
            pltpu.VMEM((2, 6, DZ, ROWS, NX), f32),
            pltpu.VMEM((2 * UP_ROWS, NX), f32),
            pltpu.VMEM((2 * DOWN_ROWS, NX), f32),
            pltpu.VMEM((16, NX), f32),
            pltpu.VMEM((16, NX), f32),
            pltpu.VMEM((8, NX), f32),
            pltpu.VMEM((8, NX), f32),
            pltpu.VMEM((16, NX), f32),
            pltpu.VMEM((8, NX), f32),
            pltpu.VMEM((8, NX), f32),
            pltpu.SemaphoreType.DMA((2, 3)),
            pltpu.SemaphoreType.DMA((2,)),
        ],
        compiler_params=params(),
        name="main",
    )(
        fp, ev, od, staged, forward_sums, adjoint_sums, inv, design,
    )
    od3, totals = lax.optimization_barrier((od3, totals))
    totals = totals + arriving
    od3 = swap(od3, "space", odd_pairs)
    totals = fold(totals, 8)
    totals = fold(totals, 24)
    totals = fold(totals, 3)
    ev3 = swap(lax.dynamic_update_slice(ev3, totals, (4, 512)), "space", even_pairs)

    norm = math.sqrt(NZ * grid_rows)

    def final(*refs):
        final_kernel(norm, *refs)

    *blocks, merit = pl.pallas_call(
        final,
        out_shape=[shaped(ROWS, width)] * groups + [shaped(1, 128)],
        in_specs=[SMEM_SPEC] + [VMEM_SPEC] * 5,
        out_specs=[VMEM_SPEC] * (groups + 1),
        scratch_shapes=[pltpu.VMEM((8, NX), f32)],
        compiler_params=params(),
        name="final",
    )(fp, ev3, od3, s_own, p_own, totals)
    block = blocks[0]
    for k in reversed(range(1, groups)):
        block = block + swap(blocks[k], "exc", [(i, i ^ k) for i in range(groups)])
    return block.T, merit[0, 0:1]


def solution(mesh):
    in_specs = (
        P("exc", None, None, "space", None),
        P("exc", None, None, "space", None),
        P("exc", None, None, "space", None),
        P("exc", None, None, "space", None),
        P("exc", None, None, "space"),
        P("exc", "space"),
        P("space", None),
        P("exc"),
        P("exc"),
        P("exc"),
        P("exc"),
        P("exc"),
    )
    out_specs = (P("exc", "space"), P("exc"))
    return jax.shard_map(local, mesh=mesh, in_specs=in_specs, out_specs=out_specs, check_vma=False)
```
